256 devices in a mesh: gx: 16 (over y, x), gy: 16 (over z, core).
Axes of the slice: x: 4, y: 4, z: 8, core: 2. Of those that a mesh axis runs over, the one named last changes fastest.
Arguments:
- load: float32 [3, 256, 256, 128], P(None, 'gx', 'gy'), may hold values from -8 to 8
- modulus: float32 [256, 256, 128], P('gx', 'gy'), may hold values from 0.5 to 5
- anchor: float32 [256, 256, 128], P('gx', 'gy'), may hold values from 0.05 to 0.5
- wall_mask: int32 [64, 64, 16], P('gx', 'gy'), may hold values 0 or 1
Outputs:
- solution: float32 [3, 256, 256, 128], P(None, 'gx', 'gy')
- remainder: float32 [3, 256, 256, 128], P(None, 'gx', 'gy')
The draws below stay inside these ranges and needn't reach their ends.
All inputs are finite; a program needn't handle non-finite values. No bound on the sum of `wall_mask` on one device may be relied on, other than what follows from the above.
Results may differ from the reference program's by a relative error of at most 0.00027.
Values sent between devices are 32-bit elements; how exact they have to be, the bound alone decides.
A program may use at most 128 MiB of HBM per device.

```python
import math
import jax
import jax.numpy as jnp

SMOOTH = 3
COARSE_STEPS = 8
NX = 256
NY = 256
NZ = 128


def with_ends(array, stream_key, low, high):
    longest = array.shape.index(max(array.shape))
    spots = []
    for shift in (0, 1):
        where = [jax.random.randint(jax.random.fold_in(stream_key, axis), (), 0, length) for axis, length in enumerate(array.shape)]
        where[longest] = (where[longest] + shift) % array.shape[longest]
        spots.append(tuple(where))
    return array.at[spots[0]].set(low).at[spots[1]].set(high)


def block_levels(key, shape, split, least, high):
    factor_of, own = 1.0, jax.random.fold_in(key, 6)
    for dim, shards_of in split:
        heights = jnp.exp(jax.random.uniform(jax.random.fold_in(own, dim), (shards_of,), jnp.float32, least / len(split), high / len(split)))
        factor_of = factor_of * jnp.repeat(heights, shape[dim] // shards_of).reshape([-1 if axis == dim else 1 for axis in range(len(shape))])
    return factor_of


def scatter_about(key, extent, width, reach, shards=(), kind=jnp.bfloat16):
    factor_of = block_levels(key, extent, shards, -0.22, 0.18) if shards else 1.0
    values = jax.random.normal(key, extent, jnp.float32) * width * factor_of
    return jnp.minimum(jnp.maximum(values, -reach), reach).astype(kind)


def setup_inputs(seed: int = 0) -> dict:
    splits = jax.random.split(jax.random.key(seed), 5)
    return {
        "load": scatter_about(splits[0], (3, NX, NY, NZ), 1.0, 8.0, ((1, 16), (2, 16)), jnp.float32),
        "modulus": jnp.clip(jnp.exp(math.log(5.0) - 2.3025851 * jax.random.uniform(splits[1], (NX, NY, NZ), jnp.float32) ** block_levels(splits[1], (NX, NY, NZ), ((0, 16), (1, 16)), -0.2, 0.2)), 0.5, 5.0),
        "anchor": jnp.clip(jnp.exp(math.log(0.5) - 2.3025851 * jax.random.uniform(splits[2], (NX, NY, NZ), jnp.float32) ** block_levels(splits[2], (NX, NY, NZ), ((0, 16), (1, 16)), -0.2, 0.2)), 0.05, 0.5),
        "wall_mask": with_ends((jax.random.randint(splits[3], (NX // 4, NY // 4, NZ // 8), 0, 2) < 1).astype(jnp.int32), jax.random.fold_in(splits[3], 1), 0, 1),
    }


def operate(field, stiff, shift):
    padded = jnp.pad(field, ((0, 0), (1, 1), (1, 1), (1, 1)))
    beside = padded[:, 2:, 1:-1, 1:-1] + padded[:, :-2, 1:-1, 1:-1]
    beside = beside + padded[:, 1:-1, 2:, 1:-1] + padded[:, 1:-1, :-2, 1:-1]
    beside = beside + padded[:, 1:-1, 1:-1, 2:] + padded[:, 1:-1, 1:-1, :-2]
    return shift * field + stiff * (6.0 * field - beside)


def chebyshev(rhs, guess, steps, low, high, stiff, shift, from_zero):
    theta = (high + low) / 2.0
    delta = (high - low) / 2.0
    sigma = theta / delta
    rho = 1.0 / sigma
    diagonal = shift + 6.0 * stiff
    resid = rhs if from_zero else rhs - operate(guess, stiff, shift)
    update = resid / (diagonal * theta)
    guess = guess + update
    for step in range(steps - 1):
        resid = rhs - operate(guess, stiff, shift)
        rho_next = 1.0 / (2.0 * sigma - rho)
        update = rho_next * rho * update + (2.0 * rho_next / delta) * resid / diagonal
        guess = guess + update
        rho = rho_next
    return guess


def boxes(field):
    shape = field.shape
    lead = shape[:-3]
    grouped = field.reshape(lead + (shape[-3] // 2, 2, shape[-2] // 2, 2, shape[-1] // 2, 2))
    count = len(lead)
    return grouped.mean(axis=(count + 1, count + 3, count + 5))


def spread_up(field):
    return jnp.repeat(jnp.repeat(jnp.repeat(field, 2, axis=-3), 2, axis=-2), 2, axis=-1)


def reference(load, modulus, anchor, wall_mask):
    blocks = jnp.repeat(jnp.repeat(jnp.repeat(wall_mask, 4, axis=0), 4, axis=1), 8, axis=2)
    stiff = modulus * (0.2 + blocks.astype(jnp.float32))
    zeros = jnp.zeros_like(load)
    pre = chebyshev(load, zeros, SMOOTH, 0.5, 2.0, stiff, anchor, True)
    fine_rest = load - operate(pre, stiff, anchor)
    coarse_rest = boxes(fine_rest)
    coarse_stiff = boxes(stiff) / 4.0
    coarse_shift = boxes(anchor)
    coarse_fix = chebyshev(coarse_rest, jnp.zeros_like(coarse_rest), COARSE_STEPS, 0.05, 2.0, coarse_stiff, coarse_shift, True)
    guess = pre + spread_up(coarse_fix)
    solution = chebyshev(load, guess, SMOOTH, 0.5, 2.0, stiff, anchor, False)
    remainder = load - operate(solution, stiff, anchor)
    return solution, remainder
```

```python
import functools
import jax
import jax.numpy as jnp
from jax import lax
from jax.experimental import pallas as pl
from jax.experimental.pallas import tpu as pltpu
from jax.sharding import PartitionSpec as P

SMOOTH = 3
COARSE_STEPS = 8
MESH = pl.DeviceIdType.MESH

NEAR = [(-1, 0), (1, 0), (0, -1), (0, 1), (-1, -1), (-1, 1), (1, -1), (1, 1)]
FAR = [(-2, 0), (2, 0), (0, -2), (0, 2)]
KNIGHT = [(s * a, t * b) for a, b in ((2, 1), (1, 2)) for s in (-1, 1) for t in (-1, 1)]
ALL = NEAR + FAR + KNIGHT


def rates(low, high, steps):
    theta, delta = (high + low) / 2.0, (high - low) / 2.0
    sigma = theta / delta
    rho = 1.0 / sigma
    out = []
    for _ in range(steps - 1):
        rho_next = 1.0 / (2.0 * sigma - rho)
        out.append((rho_next * rho, 2.0 * rho_next / delta))
        rho = rho_next
    return theta, out


def around(src, planes, rows, ends, fold):
    x, (r0, n) = planes, rows
    first, last = ends
    v = src[0:3, x, r0 : r0 + n, :]
    below = src[0:3, x - 1, r0 : r0 + n, :]
    above = pltpu.roll(v, 64, 2) if fold else src[0:3, x + 1, r0 : r0 + n, :]
    nb = jnp.where(first, 0.0, pltpu.roll(v, 1, 2)) + jnp.where(last, 0.0, pltpu.roll(v, 127, 2))
    nb = nb + (below + above)
    nb = nb + (src[0:3, x, r0 - 1 : r0 + n - 1, :] + src[0:3, x, r0 + 1 : r0 + n + 1, :])
    return v, nb


def sweep(dst, src, prev, rhs, stiff, coefs, planes, rows, ends, fold_at=None):
    cv, cn, cb, cp = coefs
    r0, n = rows
    for x in planes:
        v, nb = around(src, x, rows, ends, x == fold_at)
        out = cv * v + (cn * stiff(x, r0, n))[None] * nb
        if cb:
            out = out + cb * rhs[0:3, x, r0 : r0 + n, :]
        if prev is not None:
            out = out + cp * prev[0:3, x, r0 : r0 + n, :]
        dst[0:3, x, r0 : r0 + n, :] = out


def kernel(
    nx, ny, load, modulus, anchor, mask, out_sol, out_rem,
    f_load, f_mod, f_anc, BK, XA, XC, DG, RM, SY, RY, SC, RC, SPY, RPY, SPC, RPC,
    ZC, LC, ZR, LH, IDC, PB, PK, Q, CB, CK, CX, CY, RB, RK, R2, RY2, RN, RM2, ZF,
    in_sem, out_sem, s1, r1, sk, rk, s2, r2, sp, rp,
):
    ix, iy = lax.axis_index("gx"), lax.axis_index("gy")

    def there(d):
        conds = []
        if d[0] < 0:
            conds.append(ix >= -d[0])
        if d[0] > 0:
            conds.append(ix < nx - d[0])
        if d[1] < 0:
            conds.append(iy >= -d[1])
        if d[1] > 0:
            conds.append(iy < ny - d[1])
        return functools.reduce(jnp.logical_and, conds)

    def device(d):
        return (ix + d[0], iy + d[1])

    def opposite(d):
        return (-d[0], -d[1])

    barrier = pltpu.get_barrier_semaphore()
    for d in ALL:

        @pl.when(there(d))
        def _():
            pl.semaphore_signal(barrier, inc=1, device_id=device(d), device_id_type=MESH)

    fetch = [
        pltpu.make_async_copy(modulus, f_mod, in_sem.at[0]),
        pltpu.make_async_copy(anchor, f_anc, in_sem.at[1]),
        pltpu.make_async_copy(load, f_load, in_sem.at[2]),
    ]
    for copy in fetch:
        copy.start()

    def lo_hi(s):
        return 0 if s < 0 else 1

    def first_from(d):
        if d[1] == 0:
            return BK.at[:, 1:4, 8:24, :] if d[0] < 0 else BK.at[:, 20:23, 8:24, :]
        if d[0] == 0:
            return RY.at[lo_hi(d[1])]
        return RC.at[2 * lo_hi(d[0]) + lo_hi(d[1])]

    def first_to(d):
        if d[1] == 0:
            return BK.at[:, 4:7, 8:24, :] if d[0] < 0 else BK.at[:, 17:20, 8:24, :]
        if d[0] == 0:
            return SY.at[lo_hi(d[1])]
        return SC.at[2 * lo_hi(d[0]) + lo_hi(d[1])]

    def pre_from(d):
        if d[1] == 0:
            return XC.at[:, 0:3, 8:24, :] if d[0] < 0 else XC.at[:, 21:24, 8:24, :]
        if d[0] == 0:
            return RPY.at[lo_hi(d[1])]
        return RPC.at[2 * lo_hi(d[0]) + lo_hi(d[1])]

    def pre_to(d):
        if d[1] == 0:
            return XC.at[:, 5:8, 8:24, :] if d[0] < 0 else XC.at[:, 16:19, 8:24, :]
        if d[0] == 0:
            return SPY.at[lo_hi(d[1])]
        return SPC.at[2 * lo_hi(d[0]) + lo_hi(d[1])]

    def stiff_from(d):
        if d[0] == 0:
            return CK.at[10:14, 8:16, :] if d[1] < 0 else CK.at[10:14, 24:32, :]
        return RK.at[lo_hi(d[0]), d[1] + 1]

    def stiff_to(d):
        return PK

    def coarse_from(d):
        if abs(d[0]) < 2 and abs(d[1]) < 2:
            if d[0] == 0:
                return CB.at[:, 10:14, 8:16, :] if d[1] < 0 else CB.at[:, 10:14, 24:32, :]
            return RB.at[lo_hi(d[0]), d[1] + 1]
        if d[1] == 0:
            return R2.at[lo_hi(d[0])]
        if d[0] == 0:
            return RY2.at[lo_hi(d[1])]
        if abs(d[0]) == 2:
            return RN.at[lo_hi(d[0]), lo_hi(d[1])]
        return RM2.at[lo_hi(d[0]), lo_hi(d[1])]

    def coarse_to(d):
        if abs(d[0]) < 2 and abs(d[1]) < 2:
            return PB
        if d[1] == 0:
            return PB.at[:, 0]
        if d[0] == 0:
            return Q.at[lo_hi(d[1])]
        return Q.at[lo_hi(d[1]), 0]

    def exchange(partners, to, came, send, recv):
        def copy(k, d):
            return pltpu.make_async_remote_copy(
                src_ref=to(d), dst_ref=came(opposite(d)), send_sem=send.at[k], recv_sem=recv.at[k],
                device_id=device(d), device_id_type=MESH,
            )

        def start():
            for k, d in enumerate(partners):

                @pl.when(there(d))
                def _():
                    copy(k, d).start()

        def wait():
            for k, d in enumerate(partners):

                @pl.when(there(opposite(d)))
                def _():
                    copy(k, d).wait_recv()

        def drain():
            for k, d in enumerate(partners):

                @pl.when(there(d))
                def _():
                    copy(k, d).wait_send()

        return start, wait, drain

    one = exchange(NEAR, first_to, first_from, s1, r1)
    pre = exchange(NEAR, pre_to, pre_from, sp, rp)
    kay = exchange(NEAR, stiff_to, stiff_from, sk, rk)
    two = exchange(ALL, coarse_to, coarse_from, s2, r2)

    for partners, came in ((NEAR, first_from), (NEAR, pre_from), (NEAR, stiff_from), (ALL, coarse_from)):
        for d in partners:

            @pl.when(jnp.logical_not(there(d)))
            def _():
                place = came(d)
                place[...] = jnp.zeros(place.shape, jnp.float32)

    spread = (
        lax.broadcasted_iota(jnp.int32, (16, 128), 1) // 8 == lax.broadcasted_iota(jnp.int32, (16, 128), 0)
    ).astype(jnp.float32)
    rows4 = (
        lax.broadcasted_iota(jnp.int32, (16, 4), 0) // 4 == lax.broadcasted_iota(jnp.int32, (16, 4), 1)
    ).astype(jnp.float32)
    fetch[0].wait()
    fetch[1].wait()
    for b in range(4):
        wall = jnp.dot(mask[b].astype(jnp.float32), spread, preferred_element_type=jnp.float32)
        wall = jnp.dot(rows4, wall, preferred_element_type=jnp.float32)
        for x in range(4 * b, 4 * b + 4):
            stiff = f_mod[x] * (0.2 + wall)
            diag = f_anc[x] + 6.0 * stiff
            inv = 1.0 / diag
            DG[0, x] = diag
            DG[1, x] = inv
            BK[3, 4 + x, 8:24, :] = stiff * inv
            f_mod[x] = stiff
    fetch[2].wait()
    for x in range(16):
        BK[0:3, 4 + x, 8:24, :] = f_load[:, x] * DG[1, x][None]
    for x in range(16):
        SY[0, :, x] = BK[:, 4 + x, 8:12, :]
        SY[1, :, x] = BK[:, 4 + x, 20:24, :]
    for cx, x0 in ((0, 4), (1, 18)):
        SC[2 * cx] = BK[:, x0 : x0 + 2, 8:12, :]
        SC[2 * cx + 1] = BK[:, x0 : x0 + 2, 20:24, :]

    pl.semaphore_wait(barrier, sum(there(d).astype(jnp.int32) for d in ALL))
    one[0]()

    pair_sum = 0.125 * (
        lax.broadcasted_iota(jnp.int32, (256, 128), 0) // 2 == lax.broadcasted_iota(jnp.int32, (256, 128), 1)
    ).astype(jnp.float32)

    def gather_pairs(place, lhs, f):
        for c in range(8):
            v = place[f, c, pl.ds(0, 8, 2), :] + place[f, c, pl.ds(1, 8, 2), :]
            if c < 4:
                lhs[f, c, :, 0:128] = v
            else:
                lhs[f, 7 - c, :, 128:256] = v

    def boxes(lhs, count):
        flat = lhs[...].reshape(count * 32, 256)
        return jnp.dot(flat, pair_sum, precision=lax.Precision.HIGHEST, preferred_element_type=jnp.float32)

    for c in range(8):
        ZC[0, c] = f_mod[2 * c] + f_mod[2 * c + 1]
        ZC[1, c] = f_anc[2 * c] + f_anc[2 * c + 1]
    gather_pairs(ZC, LC, 0)
    gather_pairs(ZC, LC, 1)
    means = boxes(LC, 2)
    coarse_stiff = 0.25 * means[0:32]
    inv = 1.0 / (means[32:64] + 6.0 * coarse_stiff)
    IDC[...] = inv.reshape(4, 8, 128)
    coarse_k = (coarse_stiff * inv).reshape(4, 8, 128)
    PK[...] = coarse_k
    CK[10:14, 16:24, :] = coarse_k
    kay[0]()

    lane = lax.broadcasted_iota(jnp.int32, (3, 24, 128), 2)
    ends = (lane == 0, lane == 127)
    short = (ends[0][:, :16], ends[1][:, :16])
    theta, ((a1, b1), (a2, b2)) = rates(0.5, 2.0, SMOOTH)

    def fine_k(x, r0, n):
        return BK[3, x, r0 : r0 + n, :]

    one[1]()
    for x in range(16):
        BK[:, 4 + x, 4:8, :] = RY[0, :, x]
        BK[:, 4 + x, 24:28, :] = RY[1, :, x]
    for cx, x0 in ((0, 2), (1, 20)):
        BK[:, x0 : x0 + 2, 4:8, :] = RC[2 * cx]
        BK[:, x0 : x0 + 2, 24:28, :] = RC[2 * cx + 1]
    wide = (4, 24)
    sweep(XA, BK, None, BK, fine_k, ((1.0 + a1 - b1) / theta + b1, b1 / theta, 0.0, 0.0), range(2, 22), wide, ends)
    sweep(XC, XA, None, BK, fine_k, (1.0 + a2 - b2, b2, b2 - a2 / theta, 0.0), range(3, 21), wide, ends)

    for c in range(8):
        total = 0.0
        for x in (4 + 2 * c, 5 + 2 * c):
            v, nb = around(XC, x, (8, 16), short, False)
            total = total + DG[0, x - 4][None] * (BK[0:3, x, 8:24, :] - v + fine_k(x, 8, 16)[None] * nb)
        ZR[:, c] = total
    for f in range(3):
        gather_pairs(ZR, LH, f)
    rest = boxes(LH, 3).reshape(3, 4, 8, 128) * IDC[...][None]
    PB[...] = rest
    for j in range(4):
        Q[0, j, 0:3] = rest[:, j, 0, :]
        Q[1, j, 0:3] = rest[:, j, 7, :]
    two[0]()
    CB[:, 10:14, 16:24, :] = rest

    for x in range(16):
        SPY[0, :, x] = XC[:, 4 + x, 8:12, :]
        SPY[1, :, x] = XC[:, 4 + x, 20:24, :]
    for cx, x0 in ((0, 4), (1, 17)):
        SPC[2 * cx] = XC[:, x0 : x0 + 3, 8:12, :]
        SPC[2 * cx + 1] = XC[:, x0 : x0 + 3, 20:24, :]
    pre[0]()

    left = lax.broadcasted_iota(jnp.int32, (8, 128), 1) < 64

    def meet(lo, hi):
        return pltpu.roll(jnp.where(left[: lo.shape[-2]], hi, lo), 64, lo.ndim - 1)

    kay[1]()
    for y in range(3):
        rows = slice(8 + 8 * y, 16 + 8 * y)
        for j in range(4):
            lo, hi = RK[0, y, j], RK[1, y, j]
            CK[2 + j, rows, :] = jnp.where(left, lo, hi)
            CK[9 - j, rows, :] = meet(lo, hi)
    two[1]()
    for y in range(3):
        rows = slice(8 + 8 * y, 16 + 8 * y)
        for j in range(4):
            for f in range(3):
                lo, hi = RB[0, y, f, j], RB[1, y, f, j]
                CB[f, 2 + j, rows, :] = jnp.where(left, lo, hi)
                CB[f, 9 - j, rows, :] = meet(lo, hi)
    for f in range(3):
        CB[f, 1, 16:24, :] = meet(R2[0, f], R2[1, f])
    for y, near, far in ((0, 15, 7), (1, 24, 32)):
        near_row = meet(RN[0, y, 0:3], RN[1, y, 0:3])
        far_row = meet(RM2[0, y, 0:3], RM2[1, y, 0:3])
        for f in range(3):
            CB[f, 1, near : near + 1, :] = near_row[f : f + 1]
            CB[f, 9, far : far + 1, :] = far_row[f : f + 1]
            for j in range(4):
                CB[f, 10 + j, far : far + 1, :] = RY2[y, j, f : f + 1]

    lane = lane % 64
    ends_c = (lane == 0, lane == 63)
    short_c = (ends_c[0][:, :16], ends_c[1][:, :16])
    theta_c, steps = rates(0.05, 2.0, COARSE_STEPS)

    def coarse_k_at(x, r0, n):
        return CK[x, r0 : r0 + n, :]

    at = CB
    for t in range(2, COARSE_STEPS + 1):
        a, b = steps[t - 2]
        rows, e = ((8, 24), ends_c) if t < 6 else ((12, 16), short_c)
        to = CY if t % 2 == 0 else CX
        if t == 2:
            coefs, prev = ((1.0 + a - b) / theta_c + b, b / theta_c, 0.0, 0.0), None
        elif t == 3:
            coefs, prev = (1.0 + a - b, b, b - a / theta_c, 0.0), None
        else:
            coefs, prev = (1.0 + a - b, b, b, -a), to
        sweep(to, at, prev, CB, coarse_k_at, coefs, range(t, 14), rows, e, 13)
        at = to

    repeat = (
        lax.broadcasted_iota(jnp.int32, (128, 256), 1) // 2 == lax.broadcasted_iota(jnp.int32, (128, 256), 0)
    ).astype(jnp.float32)
    pre[1]()
    pre[2]()
    for x in range(16):
        XC[:, 4 + x, 4:8, :] = RPY[0, :, x]
        XC[:, 4 + x, 24:28, :] = RPY[1, :, x]
    for cx, x0 in ((0, 1), (1, 20)):
        XC[:, x0 : x0 + 3, 4:8, :] = RPC[2 * cx]
        XC[:, x0 : x0 + 3, 24:28, :] = RPC[2 * cx + 1]
    for f in range(3):
        for i in range(6):
            v = at[f, 8 + i, 14:26, :]
            ZF[f, i, pl.ds(0, 12, 2), :] = v
            ZF[f, i, pl.ds(1, 12, 2), :] = v
        up = jnp.dot(
            ZF[f].reshape(144, 128), repeat, precision=lax.Precision.HIGHEST, preferred_element_type=jnp.float32
        ).reshape(6, 24, 256)
        for i in range(6):
            for x, v in ((2 * i, up[i, :, 0:128]), (22 - 2 * i, up[i, :, 128:256])):
                XC[f, x, 4:28, :] = XC[f, x, 4:28, :] + v
                XC[f, x + 1, 4:28, :] = XC[f, x + 1, 4:28, :] + v

    sweep(XA, XC, None, BK, fine_k, (1.0 - 1.0 / theta, 1.0 / theta, 1.0 / theta, 0.0), range(1, 23), wide, ends)
    sweep(XC, XA, XC, BK, fine_k, (1.0 + a1 - b1, b1, b1, -a1), range(2, 22), wide, ends)
    sweep(XA, XC, XA, BK, fine_k, (1.0 + a2 - b2, b2, b2, -a2), range(3, 21), wide, ends)
    put = [
        pltpu.make_async_copy(XA.at[:, 4:20, 8:24, :], out_sol, out_sem.at[0]),
        pltpu.make_async_copy(RM, out_rem, out_sem.at[1]),
    ]
    put[0].start()
    for x in range(4, 20):
        v, nb = around(XA, x, (8, 16), short, False)
        RM[:, x - 4] = DG[0, x - 4][None] * (BK[0:3, x, 8:24, :] - v + fine_k(x, 8, 16)[None] * nb)
    put[1].start()
    for _, _, drain in (one, kay, two):
        drain()
    put[0].wait()
    put[1].wait()


def local(nx, ny, load, modulus, anchor, wall_mask):
    f32 = jnp.float32

    def vmem(*shape):
        return pltpu.VMEM(shape, f32)

    dma = pltpu.SemaphoreType.DMA
    anywhere = pl.BlockSpec(memory_space=pl.ANY)
    shape = jax.ShapeDtypeStruct((3, 16, 16, 128), f32)
    return pl.pallas_call(
        functools.partial(kernel, nx, ny),
        out_shape=(shape, shape),
        in_specs=[anywhere, anywhere, anywhere, pl.BlockSpec(memory_space=pltpu.VMEM)],
        out_specs=(anywhere, anywhere),
        scratch_shapes=[
            vmem(3, 16, 16, 128), vmem(16, 16, 128), vmem(16, 16, 128),
            vmem(4, 24, 32, 128), vmem(3, 24, 32, 128), vmem(3, 24, 32, 128),
            vmem(2, 16, 16, 128), vmem(3, 16, 16, 128),
            vmem(2, 4, 16, 4, 128), vmem(2, 4, 16, 4, 128), vmem(4, 4, 2, 4, 128), vmem(4, 4, 2, 4, 128),
            vmem(2, 3, 16, 4, 128), vmem(2, 3, 16, 4, 128), vmem(4, 3, 3, 4, 128), vmem(4, 3, 3, 4, 128),
            vmem(2, 8, 16, 128), vmem(2, 4, 8, 256), vmem(3, 8, 16, 128), vmem(3, 4, 8, 256),
            vmem(4, 8, 128), vmem(3, 4, 8, 128), vmem(4, 8, 128), vmem(2, 4, 4, 128),
            vmem(3, 14, 40, 128), vmem(14, 40, 128), vmem(3, 14, 40, 128), vmem(3, 14, 40, 128),
            vmem(2, 3, 3, 4, 8, 128), vmem(2, 3, 4, 8, 128), vmem(2, 3, 8, 128),
            vmem(2, 4, 4, 128), vmem(2, 2, 4, 128), vmem(2, 2, 4, 128),
            vmem(3, 6, 24, 128),
            dma((3,)), dma((2,)), dma((8,)), dma((8,)), dma((8,)), dma((8,)), dma((20,)), dma((20,)), dma((8,)), dma((8,)),
        ],
        compiler_params=pltpu.CompilerParams(collective_id=0, has_side_effects=True, vmem_limit_bytes=48 << 20),
    )(load, modulus, anchor, wall_mask)


def solution(mesh):
    return jax.shard_map(
        functools.partial(local, mesh.shape["gx"], mesh.shape["gy"]),
        mesh=mesh,
        in_specs=(
            P(None, "gx", "gy", None),
            P("gx", "gy", None),
            P("gx", "gy", None),
            P("gx", "gy", None),
        ),
        out_specs=(P(None, "gx", "gy", None), P(None, "gx", "gy", None)),
        check_vma=False,
    )
```

```python
import functools
import jax
import jax.numpy as jnp
from jax import lax
from jax.experimental import pallas as pl
from jax.experimental.pallas import tpu as pltpu
from jax.sharding import PartitionSpec as P

SMOOTH = 3
COARSE_STEPS = 8
MESH = pl.DeviceIdType.MESH

NEAR = [(-1, 0), (1, 0), (0, -1), (0, 1), (-1, -1), (-1, 1), (1, -1), (1, 1)]
FAR = [(-2, 0), (2, 0), (0, -2), (0, 2)]
KNIGHT = [(s * a, t * b) for a, b in ((2, 1), (1, 2)) for s in (-1, 1) for t in (-1, 1)]
ALL = NEAR + FAR + KNIGHT


def rates(low, high, steps):
    theta, delta = (high + low) / 2.0, (high - low) / 2.0
    sigma = theta / delta
    rho = 1.0 / sigma
    out = []
    for _ in range(steps - 1):
        rho_next = 1.0 / (2.0 * sigma - rho)
        out.append((rho_next * rho, 2.0 * rho_next / delta))
        rho = rho_next
    return theta, out


def around(src, planes, rows, ends, fold):
    x, (r0, n) = planes, rows
    first, last = ends
    v = src[0:3, x, r0 : r0 + n, :]
    below = src[0:3, x - 1, r0 : r0 + n, :]
    above = pltpu.roll(v, 64, 2) if fold else src[0:3, x + 1, r0 : r0 + n, :]
    nb = jnp.where(first, 0.0, pltpu.roll(v, 1, 2)) + jnp.where(last, 0.0, pltpu.roll(v, 127, 2))
    nb = nb + (below + above)
    nb = nb + (src[0:3, x, r0 - 1 : r0 + n - 1, :] + src[0:3, x, r0 + 1 : r0 + n + 1, :])
    return v, nb


def sweep(dst, src, prev, rhs, stiff, coefs, planes, rows, ends, fold_at=None):
    cv, cn, cb, cp = coefs
    r0, n = rows
    for x in planes:
        v, nb = around(src, x, rows, ends, x == fold_at)
        out = cv * v + (cn * stiff(x, r0, n))[None] * nb
        if cb:
            out = out + cb * rhs[0:3, x, r0 : r0 + n, :]
        if prev is not None:
            out = out + cp * prev[0:3, x, r0 : r0 + n, :]
        dst[0:3, x, r0 : r0 + n, :] = out


def kernel(
    nx, ny, load, modulus, anchor, wall_mask, XC, BK, DG,
    f_load, f_mod, f_anc, mask, INV, XA, SY, RY, SC, RC, SPY, RPY, SPC, RPC,
    ZC, LC, ZR, LH, IDC, PB, PK, Q, CB, CK, CX, CY, RB, RK, R2, RY2, RN, RM2, ZF,
    in_sem, s1, r1, sk, rk, s2, r2, sp, rp,
):
    ix, iy = lax.axis_index("gx"), lax.axis_index("gy")

    def there(d):
        conds = []
        if d[0] < 0:
            conds.append(ix >= -d[0])
        if d[0] > 0:
            conds.append(ix < nx - d[0])
        if d[1] < 0:
            conds.append(iy >= -d[1])
        if d[1] > 0:
            conds.append(iy < ny - d[1])
        return functools.reduce(jnp.logical_and, conds)

    def device(d):
        return (ix + d[0], iy + d[1])

    def opposite(d):
        return (-d[0], -d[1])

    barrier = pltpu.get_barrier_semaphore()
    for d in ALL:

        @pl.when(there(d))
        def _():
            pl.semaphore_signal(barrier, inc=1, device_id=device(d), device_id_type=MESH)

    fetch = [
        pltpu.make_async_copy(modulus, f_mod, in_sem.at[0]),
        pltpu.make_async_copy(anchor, f_anc, in_sem.at[1]),
        pltpu.make_async_copy(wall_mask, mask, in_sem.at[2]),
        pltpu.make_async_copy(load, f_load, in_sem.at[3]),
    ]
    for copy in fetch:
        copy.start()

    def lo_hi(s):
        return 0 if s < 0 else 1

    def first_from(d):
        if d[1] == 0:
            return BK.at[:, 1:4, 8:24, :] if d[0] < 0 else BK.at[:, 20:23, 8:24, :]
        if d[0] == 0:
            return RY.at[lo_hi(d[1])]
        return RC.at[2 * lo_hi(d[0]) + lo_hi(d[1])]

    def first_to(d):
        if d[1] == 0:
            return BK.at[:, 4:7, 8:24, :] if d[0] < 0 else BK.at[:, 17:20, 8:24, :]
        if d[0] == 0:
            return SY.at[lo_hi(d[1])]
        return SC.at[2 * lo_hi(d[0]) + lo_hi(d[1])]

    def pre_from(d):
        if d[1] == 0:
            return XC.at[:, 0:3, 8:24, :] if d[0] < 0 else XC.at[:, 21:24, 8:24, :]
        if d[0] == 0:
            return RPY.at[lo_hi(d[1])]
        return RPC.at[2 * lo_hi(d[0]) + lo_hi(d[1])]

    def pre_to(d):
        if d[1] == 0:
            return XC.at[:, 5:8, 8:24, :] if d[0] < 0 else XC.at[:, 16:19, 8:24, :]
        if d[0] == 0:
            return SPY.at[lo_hi(d[1])]
        return SPC.at[2 * lo_hi(d[0]) + lo_hi(d[1])]

    def stiff_from(d):
        if d[0] == 0:
            return CK.at[10:14, 8:16, :] if d[1] < 0 else CK.at[10:14, 24:32, :]
        return RK.at[lo_hi(d[0]), d[1] + 1]

    def stiff_to(d):
        return PK

    def coarse_from(d):
        if abs(d[0]) < 2 and abs(d[1]) < 2:
            if d[0] == 0:
                return CB.at[:, 10:14, 8:16, :] if d[1] < 0 else CB.at[:, 10:14, 24:32, :]
            return RB.at[lo_hi(d[0]), d[1] + 1]
        if d[1] == 0:
            return R2.at[lo_hi(d[0])]
        if d[0] == 0:
            return RY2.at[lo_hi(d[1])]
        if abs(d[0]) == 2:
            return RN.at[lo_hi(d[0]), lo_hi(d[1])]
        return RM2.at[lo_hi(d[0]), lo_hi(d[1])]

    def coarse_to(d):
        if abs(d[0]) < 2 and abs(d[1]) < 2:
            return PB
        if d[1] == 0:
            return PB.at[:, 0]
        if d[0] == 0:
            return Q.at[lo_hi(d[1])]
        return Q.at[lo_hi(d[1]), 0]

    def exchange(partners, to, came, send, recv):
        def copy(k, d):
            return pltpu.make_async_remote_copy(
                src_ref=to(d), dst_ref=came(opposite(d)), send_sem=send.at[k], recv_sem=recv.at[k],
                device_id=device(d), device_id_type=MESH,
            )

        def start():
            for k, d in enumerate(partners):

                @pl.when(there(d))
                def _():
                    copy(k, d).start()

        def wait():
            for k, d in enumerate(partners):

                @pl.when(there(opposite(d)))
                def _():
                    copy(k, d).wait_recv()

        def drain():
            for k, d in enumerate(partners):

                @pl.when(there(d))
                def _():
                    copy(k, d).wait_send()

        return start, wait, drain

    one = exchange(NEAR, first_to, first_from, s1, r1)
    pre = exchange(NEAR, pre_to, pre_from, sp, rp)
    kay = exchange(NEAR, stiff_to, stiff_from, sk, rk)
    two = exchange(ALL, coarse_to, coarse_from, s2, r2)

    for partners, came in ((NEAR, first_from), (NEAR, pre_from), (NEAR, stiff_from), (ALL, coarse_from)):
        for d in partners:

            @pl.when(jnp.logical_not(there(d)))
            def _():
                place = came(d)
                place[...] = jnp.zeros(place.shape, jnp.float32)

    spread = (
        lax.broadcasted_iota(jnp.int32, (16, 128), 1) // 8 == lax.broadcasted_iota(jnp.int32, (16, 128), 0)
    ).astype(jnp.float32)
    rows4 = (
        lax.broadcasted_iota(jnp.int32, (16, 4), 0) // 4 == lax.broadcasted_iota(jnp.int32, (16, 4), 1)
    ).astype(jnp.float32)
    fetch[0].wait()
    fetch[1].wait()
    fetch[2].wait()
    for b in range(4):
        wall = jnp.dot(mask[b].astype(jnp.float32), spread, preferred_element_type=jnp.float32)
        wall = jnp.dot(rows4, wall, preferred_element_type=jnp.float32)
        for x in range(4 * b, 4 * b + 4):
            stiff = f_mod[x] * (0.2 + wall)
            diag = f_anc[x] + 6.0 * stiff
            inv = 1.0 / diag
            DG[x] = diag
            INV[x] = inv
            BK[3, 4 + x, 8:24, :] = stiff * inv
            f_mod[x] = stiff
    fetch[3].wait()
    for x in range(16):
        BK[0:3, 4 + x, 8:24, :] = f_load[:, x] * INV[x][None]
    for x in range(16):
        SY[0, :, x] = BK[:, 4 + x, 8:12, :]
        SY[1, :, x] = BK[:, 4 + x, 20:24, :]
    for cx, x0 in ((0, 4), (1, 18)):
        SC[2 * cx] = BK[:, x0 : x0 + 2, 8:12, :]
        SC[2 * cx + 1] = BK[:, x0 : x0 + 2, 20:24, :]

    pl.semaphore_wait(barrier, sum(there(d).astype(jnp.int32) for d in ALL))
    one[0]()

    pair_sum = 0.125 * (
        lax.broadcasted_iota(jnp.int32, (256, 128), 0) // 2 == lax.broadcasted_iota(jnp.int32, (256, 128), 1)
    ).astype(jnp.float32)

    def gather_pairs(place, lhs, f):
        for c in range(8):
            v = place[f, c, pl.ds(0, 8, 2), :] + place[f, c, pl.ds(1, 8, 2), :]
            if c < 4:
                lhs[f, c, :, 0:128] = v
            else:
                lhs[f, 7 - c, :, 128:256] = v

    def boxes(lhs, count):
        flat = lhs[...].reshape(count * 32, 256)
        return jnp.dot(flat, pair_sum, precision=lax.Precision.HIGHEST, preferred_element_type=jnp.float32)

    for c in range(8):
        ZC[0, c] = f_mod[2 * c] + f_mod[2 * c + 1]
        ZC[1, c] = f_anc[2 * c] + f_anc[2 * c + 1]
    gather_pairs(ZC, LC, 0)
    gather_pairs(ZC, LC, 1)
    means = boxes(LC, 2)
    coarse_stiff = 0.25 * means[0:32]
    inv = 1.0 / (means[32:64] + 6.0 * coarse_stiff)
    IDC[...] = inv.reshape(4, 8, 128)
    coarse_k = (coarse_stiff * inv).reshape(4, 8, 128)
    PK[...] = coarse_k
    CK[10:14, 16:24, :] = coarse_k
    kay[0]()

    lane = lax.broadcasted_iota(jnp.int32, (3, 24, 128), 2)
    ends = (lane == 0, lane == 127)
    short = (ends[0][:, :16], ends[1][:, :16])
    theta, ((a1, b1), (a2, b2)) = rates(0.5, 2.0, SMOOTH)

    def fine_k(x, r0, n):
        return BK[3, x, r0 : r0 + n, :]

    one[1]()
    for x in range(16):
        BK[:, 4 + x, 4:8, :] = RY[0, :, x]
        BK[:, 4 + x, 24:28, :] = RY[1, :, x]
    for cx, x0 in ((0, 2), (1, 20)):
        BK[:, x0 : x0 + 2, 4:8, :] = RC[2 * cx]
        BK[:, x0 : x0 + 2, 24:28, :] = RC[2 * cx + 1]
    wide = (4, 24)
    sweep(XA, BK, None, BK, fine_k, ((1.0 + a1 - b1) / theta + b1, b1 / theta, 0.0, 0.0), range(2, 22), wide, ends)
    sweep(XC, XA, None, BK, fine_k, (1.0 + a2 - b2, b2, b2 - a2 / theta, 0.0), range(3, 21), wide, ends)

    for c in range(8):
        total = 0.0
        for x in (4 + 2 * c, 5 + 2 * c):
            v, nb = around(XC, x, (8, 16), short, False)
            total = total + DG[x - 4][None] * (BK[0:3, x, 8:24, :] - v + fine_k(x, 8, 16)[None] * nb)
        ZR[:, c] = total
    for f in range(3):
        gather_pairs(ZR, LH, f)
    rest = boxes(LH, 3).reshape(3, 4, 8, 128) * IDC[...][None]
    PB[...] = rest
    for j in range(4):
        Q[0, j, 0:3] = rest[:, j, 0, :]
        Q[1, j, 0:3] = rest[:, j, 7, :]
    two[0]()
    CB[:, 10:14, 16:24, :] = rest

    for x in range(16):
        SPY[0, :, x] = XC[:, 4 + x, 8:12, :]
        SPY[1, :, x] = XC[:, 4 + x, 20:24, :]
    for cx, x0 in ((0, 4), (1, 17)):
        SPC[2 * cx] = XC[:, x0 : x0 + 3, 8:12, :]
        SPC[2 * cx + 1] = XC[:, x0 : x0 + 3, 20:24, :]
    pre[0]()

    left = lax.broadcasted_iota(jnp.int32, (8, 128), 1) < 64

    def meet(lo, hi):
        return pltpu.roll(jnp.where(left[: lo.shape[-2]], hi, lo), 64, lo.ndim - 1)

    kay[1]()
    for y in range(3):
        rows = slice(8 + 8 * y, 16 + 8 * y)
        for j in range(4):
            lo, hi = RK[0, y, j], RK[1, y, j]
            CK[2 + j, rows, :] = jnp.where(left, lo, hi)
            CK[9 - j, rows, :] = meet(lo, hi)
    two[1]()
    for y in range(3):
        rows = slice(8 + 8 * y, 16 + 8 * y)
        for j in range(4):
            for f in range(3):
                lo, hi = RB[0, y, f, j], RB[1, y, f, j]
                CB[f, 2 + j, rows, :] = jnp.where(left, lo, hi)
                CB[f, 9 - j, rows, :] = meet(lo, hi)
    for f in range(3):
        CB[f, 1, 16:24, :] = meet(R2[0, f], R2[1, f])
    for y, near, far in ((0, 15, 7), (1, 24, 32)):
        near_row = meet(RN[0, y, 0:3], RN[1, y, 0:3])
        far_row = meet(RM2[0, y, 0:3], RM2[1, y, 0:3])
        for f in range(3):
            CB[f, 1, near : near + 1, :] = near_row[f : f + 1]
            CB[f, 9, far : far + 1, :] = far_row[f : f + 1]
            for j in range(4):
                CB[f, 10 + j, far : far + 1, :] = RY2[y, j, f : f + 1]

    lane = lane % 64
    ends_c = (lane == 0, lane == 63)
    short_c = (ends_c[0][:, :16], ends_c[1][:, :16])
    theta_c, steps = rates(0.05, 2.0, COARSE_STEPS)

    def coarse_k_at(x, r0, n):
        return CK[x, r0 : r0 + n, :]

    at = CB
    for t in range(2, COARSE_STEPS + 1):
        a, b = steps[t - 2]
        rows, e = ((8, 24), ends_c) if t < 6 else ((12, 16), short_c)
        to = CY if t % 2 == 0 else CX
        if t == 2:
            coefs, prev = ((1.0 + a - b) / theta_c + b, b / theta_c, 0.0, 0.0), None
        elif t == 3:
            coefs, prev = (1.0 + a - b, b, b - a / theta_c, 0.0), None
        else:
            coefs, prev = (1.0 + a - b, b, b, -a), to
        sweep(to, at, prev, CB, coarse_k_at, coefs, range(t, 14), rows, e, 13)
        at = to

    repeat = (
        lax.broadcasted_iota(jnp.int32, (128, 256), 1) // 2 == lax.broadcasted_iota(jnp.int32, (128, 256), 0)
    ).astype(jnp.float32)
    pre[1]()
    pre[2]()
    for x in range(16):
        XC[:, 4 + x, 4:8, :] = RPY[0, :, x]
        XC[:, 4 + x, 24:28, :] = RPY[1, :, x]
    for cx, x0 in ((0, 1), (1, 20)):
        XC[:, x0 : x0 + 3, 4:8, :] = RPC[2 * cx]
        XC[:, x0 : x0 + 3, 24:28, :] = RPC[2 * cx + 1]
    for f in range(3):
        for i in range(6):
            v = at[f, 8 + i, 14:26, :]
            ZF[f, i, pl.ds(0, 12, 2), :] = v
            ZF[f, i, pl.ds(1, 12, 2), :] = v
        up = jnp.dot(
            ZF[f].reshape(144, 128), repeat, precision=lax.Precision.HIGHEST, preferred_element_type=jnp.float32
        ).reshape(6, 24, 256)
        for i in range(6):
            for x, v in ((2 * i, up[i, :, 0:128]), (22 - 2 * i, up[i, :, 128:256])):
                XC[f, x, 4:28, :] = XC[f, x, 4:28, :] + v
                XC[f, x + 1, 4:28, :] = XC[f, x + 1, 4:28, :] + v
    for _, _, drain in (one, kay, two):
        drain()


def after(XC, BK, DG, out_sol, out_rem, XA, XB, RM, out_sem):
    lane = lax.broadcasted_iota(jnp.int32, (3, 24, 128), 2)
    ends = (lane == 0, lane == 127)
    short = (ends[0][:, :16], ends[1][:, :16])
    theta, ((a1, b1), (a2, b2)) = rates(0.5, 2.0, SMOOTH)
    wide = (4, 24)

    def fine_k(x, r0, n):
        return BK[3, x, r0 : r0 + n, :]

    sweep(XA, XC, None, BK, fine_k, (1.0 - 1.0 / theta, 1.0 / theta, 1.0 / theta, 0.0), range(1, 23), wide, ends)
    sweep(XB, XA, XC, BK, fine_k, (1.0 + a1 - b1, b1, b1, -a1), range(2, 22), wide, ends)
    sweep(XA, XB, XA, BK, fine_k, (1.0 + a2 - b2, b2, b2, -a2), range(3, 21), wide, ends)
    put = [
        pltpu.make_async_copy(XA.at[:, 4:20, 8:24, :], out_sol, out_sem.at[0]),
        pltpu.make_async_copy(RM, out_rem, out_sem.at[1]),
    ]
    put[0].start()
    for x in range(4, 20):
        v, nb = around(XA, x, (8, 16), short, False)
        RM[:, x - 4] = DG[x - 4][None] * (BK[0:3, x, 8:24, :] - v + fine_k(x, 8, 16)[None] * nb)
    put[1].start()
    put[0].wait()
    put[1].wait()


def local(nx, ny, load, modulus, anchor, wall_mask):
    f32 = jnp.float32

    def vmem(*shape):
        return pltpu.VMEM(shape, f32)

    dma = pltpu.SemaphoreType.DMA
    far = pl.BlockSpec(memory_space=pltpu.HBM)
    near = pl.BlockSpec(memory_space=pltpu.VMEM)
    inner = pl.pallas_call(
        functools.partial(kernel, nx, ny),
        out_shape=(
            jax.ShapeDtypeStruct((3, 24, 32, 128), f32),
            jax.ShapeDtypeStruct((4, 24, 32, 128), f32),
            jax.ShapeDtypeStruct((16, 16, 128), f32),
        ),
        in_specs=[far] * 4,
        out_specs=(near, near, near),
        scratch_shapes=[
            vmem(3, 16, 16, 128), vmem(16, 16, 128), vmem(16, 16, 128),
            pltpu.VMEM((4, 4, 16), jnp.int32), vmem(16, 16, 128), vmem(3, 24, 32, 128),
            vmem(2, 4, 16, 4, 128), vmem(2, 4, 16, 4, 128), vmem(4, 4, 2, 4, 128), vmem(4, 4, 2, 4, 128),
            vmem(2, 3, 16, 4, 128), vmem(2, 3, 16, 4, 128), vmem(4, 3, 3, 4, 128), vmem(4, 3, 3, 4, 128),
            vmem(2, 8, 16, 128), vmem(2, 4, 8, 256), vmem(3, 8, 16, 128), vmem(3, 4, 8, 256),
            vmem(4, 8, 128), vmem(3, 4, 8, 128), vmem(4, 8, 128), vmem(2, 4, 4, 128),
            vmem(3, 14, 40, 128), vmem(14, 40, 128), vmem(3, 14, 40, 128), vmem(3, 14, 40, 128),
            vmem(2, 3, 3, 4, 8, 128), vmem(2, 3, 4, 8, 128), vmem(2, 3, 8, 128),
            vmem(2, 4, 4, 128), vmem(2, 2, 4, 128), vmem(2, 2, 4, 128),
            vmem(3, 6, 24, 128),
            dma((4,)), dma((8,)), dma((8,)), dma((8,)), dma((8,)), dma((20,)), dma((20,)), dma((8,)), dma((8,)),
        ],
        compiler_params=pltpu.CompilerParams(collective_id=0, has_side_effects=True, vmem_limit_bytes=24 << 20),
    )(*(pltpu.with_memory_space_constraint(a, pltpu.HBM) for a in (load, modulus, anchor, wall_mask)))
    shape = jax.ShapeDtypeStruct((3, 16, 16, 128), f32)
    return pl.pallas_call(
        after,
        out_shape=(shape, shape),
        in_specs=[near] * 3,
        out_specs=(far, far),
        scratch_shapes=[vmem(3, 24, 32, 128), vmem(3, 24, 32, 128), vmem(3, 16, 16, 128), dma((2,))],
        compiler_params=pltpu.CompilerParams(vmem_limit_bytes=16 << 20),
    )(*inner)


def solution(mesh):
    return jax.shard_map(
        functools.partial(local, mesh.shape["gx"], mesh.shape["gy"]),
        mesh=mesh,
        in_specs=(
            P(None, "gx", "gy", None),
            P("gx", "gy", None),
            P("gx", "gy", None),
            P("gx", "gy", None),
        ),
        out_specs=(P(None, "gx", "gy", None), P(None, "gx", "gy", None)),
        check_vma=False,
    )
```

```python
import functools
import jax
import jax.numpy as jnp
from jax import lax
from jax.experimental import pallas as pl
from jax.experimental.pallas import tpu as pltpu
from jax.sharding import PartitionSpec as P

SMOOTH = 3
COARSE_STEPS = 8
MESH = pl.DeviceIdType.MESH

NEAR = [(-1, -1), (-1, 1), (1, -1), (1, 1), (-1, 0), (1, 0), (0, -1), (0, 1)]
FAR = [(-2, 0), (2, 0), (0, -2), (0, 2)]
KNIGHT = [(s * a, t * b) for a, b in ((2, 1), (1, 2)) for s in (-1, 1) for t in (-1, 1)]
ALL = KNIGHT + FAR + NEAR


def rates(low, high, steps):
    theta, delta = (high + low) / 2.0, (high - low) / 2.0
    sigma = theta / delta
    rho = 1.0 / sigma
    out = []
    for _ in range(steps - 1):
        rho_next = 1.0 / (2.0 * sigma - rho)
        out.append((rho_next * rho, 2.0 * rho_next / delta))
        rho = rho_next
    return theta, out


def around(src, x, rows, ends, held, fold=False):
    r0, n = rows
    first, last = ends[n]

    def plane(p):
        if (p, rows) not in held:
            held[p, rows] = src[0:3, p, r0 : r0 + n, :]
        return held[p, rows]

    below, v = plane(x - 1), plane(x)
    above = pltpu.roll(v, 64, 2) if fold else plane(x + 1)
    nb = jnp.where(first, 0.0, pltpu.roll(v, 1, 2)) + jnp.where(last, 0.0, pltpu.roll(v, 127, 2))
    nb = nb + (below + above)
    nb = nb + (src[0:3, x, r0 - 1 : r0 + n - 1, :] + src[0:3, x, r0 + 1 : r0 + n + 1, :])
    return v, nb


def sweep(dst, src, prev, rhs, stiff, coefs, planes, rows_of, ends, fold_at=None):
    cv, cn, cb, cp = coefs
    held = {}
    for x in planes:
        r0, n = rows_of(x)
        v, nb = around(src, x, (r0, n), ends, held, x == fold_at)
        out = cv * v + (cn * stiff(x, r0, n))[None] * nb
        if cb:
            out = out + cb * rhs[0:3, x, r0 : r0 + n, :]
        if prev is not None:
            out = out + cp * prev[0:3, x, r0 : r0 + n, :]
        dst[0:3, x, r0 : r0 + n, :] = out


def lane_ends(period):
    lane = lax.broadcasted_iota(jnp.int32, (3, 24, 128), 2) % period
    first, last = lane == 0, lane == period - 1
    return {24: (first, last), 16: (first[:, :16], last[:, :16])}


def fine_rows(reach):
    return lambda x: (8, 16) if x in (4 - reach, 19 + reach) else (4, 24)


def coarse_rows(step):
    def of(x):
        away = max(0, 10 - x)
        return (12, 16) if (11 - step - away if away else 10 - step) <= 4 else (8, 24)

    return of


def kernel(
    nx, ny, load, modulus, anchor, wall_mask, XC, BK, DG,
    f_load, f_mod, f_anc, mask, INV, XA, SY, RY, SC, RC, SPY, RPY, SPC, RPC,
    ZC, LC, ZR, LH, IDC, PB, PK, Q, CB, CK, CX, CY, RB, RD, PC, RK, R2, RY2, RN, RM2, ZF,
    in_sem, s1, r1, sk, rk, s2, r2, sp, rp,
):
    ix, iy = lax.axis_index("gx"), lax.axis_index("gy")

    def there(d):
        conds = []
        if d[0] < 0:
            conds.append(ix >= -d[0])
        if d[0] > 0:
            conds.append(ix < nx - d[0])
        if d[1] < 0:
            conds.append(iy >= -d[1])
        if d[1] > 0:
            conds.append(iy < ny - d[1])
        return functools.reduce(jnp.logical_and, conds)

    def device(d):
        return (ix + d[0], iy + d[1])

    def opposite(d):
        return (-d[0], -d[1])

    barrier = pltpu.get_barrier_semaphore()
    for d in ALL:

        @pl.when(there(d))
        def _():
            pl.semaphore_signal(barrier, inc=1, device_id=device(d), device_id_type=MESH)

    fetch = [
        pltpu.make_async_copy(modulus, f_mod, in_sem.at[0]),
        pltpu.make_async_copy(anchor, f_anc, in_sem.at[1]),
        pltpu.make_async_copy(wall_mask, mask, in_sem.at[2]),
        pltpu.make_async_copy(load, f_load, in_sem.at[3]),
    ]
    for copy in fetch:
        copy.start()

    def lo_hi(s):
        return 0 if s < 0 else 1

    def first_from(d):
        if d[1] == 0:
            return BK.at[:, 1:4, 8:24, :] if d[0] < 0 else BK.at[:, 20:23, 8:24, :]
        if d[0] == 0:
            return RY.at[lo_hi(d[1])]
        return RC.at[2 * lo_hi(d[0]) + lo_hi(d[1])]

    def first_to(d):
        if d[1] == 0:
            return BK.at[:, 4:7, 8:24, :] if d[0] < 0 else BK.at[:, 17:20, 8:24, :]
        if d[0] == 0:
            return SY.at[lo_hi(d[1])]
        return SC.at[2 * lo_hi(d[0]) + lo_hi(d[1])]

    def pre_from(d):
        if d[1] == 0:
            return XC.at[:, 0:3, 8:24, :] if d[0] < 0 else XC.at[:, 21:24, 8:24, :]
        if d[0] == 0:
            return RPY.at[lo_hi(d[1])]
        return RPC.at[2 * lo_hi(d[0]) + lo_hi(d[1])]

    def pre_to(d):
        if d[1] == 0:
            return XC.at[:, 5:8, 8:24, :] if d[0] < 0 else XC.at[:, 16:19, 8:24, :]
        if d[0] == 0:
            return SPY.at[lo_hi(d[1])]
        return SPC.at[2 * lo_hi(d[0]) + lo_hi(d[1])]

    def stiff_from(d):
        if d[0] == 0:
            return CK.at[10:14, 8:16, :] if d[1] < 0 else CK.at[10:14, 24:32, :]
        return RK.at[lo_hi(d[0]), d[1] + 1]

    def stiff_to(d):
        return PK

    def coarse_from(d):
        if abs(d[0]) < 2 and abs(d[1]) < 2:
            if d[0] == 0:
                return CB.at[:, 10:14, 8:16, :] if d[1] < 0 else CB.at[:, 10:14, 24:32, :]
            return RB.at[lo_hi(d[0])] if d[1] == 0 else RD.at[lo_hi(d[0]), lo_hi(d[1])]
        if d[1] == 0:
            return R2.at[lo_hi(d[0])]
        if d[0] == 0:
            return RY2.at[lo_hi(d[1])]
        if abs(d[0]) == 2:
            return RN.at[lo_hi(d[0]), lo_hi(d[1])]
        return RM2.at[lo_hi(d[0]), lo_hi(d[1])]

    def coarse_to(d):
        if abs(d[0]) < 2 and abs(d[1]) < 2:
            return PB if d[0] == 0 or d[1] == 0 else PC.at[lo_hi(d[0]), lo_hi(d[1])]
        if d[1] == 0:
            return PB.at[:, 0]
        if d[0] == 0:
            return Q.at[lo_hi(d[1])]
        return Q.at[lo_hi(d[1]), 0]

    def exchange(partners, to, came, send, recv):
        def copy(k, d):
            return pltpu.make_async_remote_copy(
                src_ref=to(d), dst_ref=came(opposite(d)), send_sem=send.at[k], recv_sem=recv.at[k],
                device_id=device(d), device_id_type=MESH,
            )

        def start():
            for k, d in enumerate(partners):

                @pl.when(there(d))
                def _():
                    copy(k, d).start()

        def wait(chosen=lambda d: True):
            for k, d in enumerate(partners):
                if not chosen(d):
                    continue

                @pl.when(there(opposite(d)))
                def _():
                    copy(k, d).wait_recv()

        def drain():
            for k, d in enumerate(partners):

                @pl.when(there(d))
                def _():
                    copy(k, d).wait_send()

        return start, wait, drain

    one = exchange(NEAR, first_to, first_from, s1, r1)
    pre = exchange(NEAR, pre_to, pre_from, sp, rp)
    kay = exchange(NEAR, stiff_to, stiff_from, sk, rk)
    two = exchange(ALL, coarse_to, coarse_from, s2, r2)

    for partners, came in ((NEAR, first_from), (NEAR, pre_from), (NEAR, stiff_from), (ALL, coarse_from)):
        for d in partners:

            @pl.when(jnp.logical_not(there(d)))
            def _():
                place = came(d)
                place[...] = jnp.zeros(place.shape, jnp.float32)

    spread = (
        lax.broadcasted_iota(jnp.int32, (16, 128), 1) // 8 == lax.broadcasted_iota(jnp.int32, (16, 128), 0)
    ).astype(jnp.float32)
    rows4 = (
        lax.broadcasted_iota(jnp.int32, (16, 4), 0) // 4 == lax.broadcasted_iota(jnp.int32, (16, 4), 1)
    ).astype(jnp.float32)
    fetch[0].wait()
    fetch[1].wait()
    fetch[2].wait()
    for b in range(4):
        wall = jnp.dot(mask[b].astype(jnp.float32), spread, preferred_element_type=jnp.float32)
        wall = jnp.dot(rows4, wall, preferred_element_type=jnp.float32)
        for x in range(4 * b, 4 * b + 4):
            stiff = f_mod[x] * (0.2 + wall)
            diag = f_anc[x] + 6.0 * stiff
            inv = 1.0 / diag
            DG[x] = diag
            INV[x] = inv
            BK[3, 4 + x, 8:24, :] = stiff * inv
            f_mod[x] = stiff
    fetch[3].wait()
    for x in range(16):
        BK[0:3, 4 + x, 8:24, :] = f_load[:, x] * INV[x][None]
    for x in range(16):
        SY[0, :, x] = BK[:, 4 + x, 8:12, :]
        SY[1, :, x] = BK[:, 4 + x, 20:24, :]
    for cx, x0 in ((0, 4), (1, 18)):
        SC[2 * cx] = BK[:, x0 : x0 + 2, 8:12, :]
        SC[2 * cx + 1] = BK[:, x0 : x0 + 2, 20:24, :]

    pl.semaphore_wait(barrier, sum(there(d).astype(jnp.int32) for d in ALL))
    one[0]()

    pair_sum = 0.125 * (
        lax.broadcasted_iota(jnp.int32, (256, 128), 0) // 2 == lax.broadcasted_iota(jnp.int32, (256, 128), 1)
    ).astype(jnp.float32)

    def gather_pairs(place, lhs, f):
        for c in range(8):
            v = place[f, c, pl.ds(0, 8, 2), :] + place[f, c, pl.ds(1, 8, 2), :]
            if c < 4:
                lhs[f, c, :, 0:128] = v
            else:
                lhs[f, 7 - c, :, 128:256] = v

    def boxes(lhs, count):
        flat = lhs[...].reshape(count * 32, 256)
        return jnp.dot(flat, pair_sum, precision=lax.Precision.HIGHEST, preferred_element_type=jnp.float32)

    for c in range(8):
        ZC[0, c] = f_mod[2 * c] + f_mod[2 * c + 1]
        ZC[1, c] = f_anc[2 * c] + f_anc[2 * c + 1]
    gather_pairs(ZC, LC, 0)
    gather_pairs(ZC, LC, 1)
    means = boxes(LC, 2)
    coarse_stiff = 0.25 * means[0:32]
    inv = 1.0 / (means[32:64] + 6.0 * coarse_stiff)
    IDC[...] = inv.reshape(4, 8, 128)
    coarse_k = (coarse_stiff * inv).reshape(4, 8, 128)
    PK[...] = coarse_k
    CK[10:14, 16:24, :] = coarse_k
    kay[0]()

    ends = lane_ends(128)
    theta, ((a1, b1), (a2, b2)) = rates(0.5, 2.0, SMOOTH)

    def fine_k(x, r0, n):
        return BK[3, x, r0 : r0 + n, :]

    def smooth(second, third, pairs):
        coefs = ((1.0 + a1 - b1) / theta + b1, b1 / theta, 0.0, 0.0)
        for planes in second:
            sweep(XA, BK, None, BK, fine_k, coefs, planes, fine_rows(2), ends)
        coefs = (1.0 + a2 - b2, b2, b2 - a2 / theta, 0.0)
        for planes in third:
            sweep(XC, XA, None, BK, fine_k, coefs, planes, fine_rows(1), ends)
        held = {}
        for c in pairs:
            total = 0.0
            for x in (4 + 2 * c, 5 + 2 * c):
                v, nb = around(XC, x, (8, 16), ends, held)
                total = total + DG[x - 4][None] * (BK[0:3, x, 8:24, :] - v + fine_k(x, 8, 16)[None] * nb)
            ZR[:, c] = total

    one[1](lambda d: d[0] == 0)
    for x in range(16):
        BK[:, 4 + x, 4:8, :] = RY[0, :, x]
        BK[:, 4 + x, 24:28, :] = RY[1, :, x]
    smooth([range(5, 19)], [range(6, 18)], range(2, 6))
    one[1](lambda d: d[0] != 0)
    for cx, x0 in ((0, 2), (1, 20)):
        BK[:, x0 : x0 + 2, 4:8, :] = RC[2 * cx]
        BK[:, x0 : x0 + 2, 24:28, :] = RC[2 * cx + 1]
    smooth([range(2, 5), range(19, 22)], [range(3, 6), range(18, 21)], (0, 1, 6, 7))

    for f in range(3):
        gather_pairs(ZR, LH, f)
    rest = boxes(LH, 3).reshape(3, 4, 8, 128) * IDC[...][None]
    PB[...] = rest
    left = lax.broadcasted_iota(jnp.int32, (8, 128), 1) < 64
    row = lax.broadcasted_iota(jnp.int32, (8, 128), 0)
    for dx in (0, 1):
        far_half = left if dx else jnp.logical_not(left)
        first_two = jnp.where(far_half, pltpu.roll(rest[:, 1], 64, 2), rest[:, 0])
        last_two = jnp.where(far_half, pltpu.roll(rest[:, 3], 64, 2), rest[:, 2])
        for dy, shift1, shift0, has1, has0 in ((0, 5, 6, row >= 5, row >= 6), (1, 3, 2, row < 3, row < 2)):
            odd = jnp.where(has1, pltpu.roll(rest[:, 1], shift1, 1), rest[:, 3])
            even = jnp.where(has0, pltpu.roll(rest[:, 0], shift0, 1), rest[:, 2])
            PC[dx, dy, 0] = first_two
            PC[dx, dy, 1] = last_two
            PC[dx, dy, 2] = jnp.where(far_half, odd, pltpu.roll(even, 64, 2))
    for j in range(4):
        Q[0, j, 0:3] = rest[:, j, 0, :]
        Q[1, j, 0:3] = rest[:, j, 7, :]
    two[0]()
    CB[:, 10:14, 16:24, :] = rest

    for x in range(16):
        SPY[0, :, x] = XC[:, 4 + x, 8:12, :]
        SPY[1, :, x] = XC[:, 4 + x, 20:24, :]
    for cx, x0 in ((0, 4), (1, 17)):
        SPC[2 * cx] = XC[:, x0 : x0 + 3, 8:12, :]
        SPC[2 * cx + 1] = XC[:, x0 : x0 + 3, 20:24, :]
    pre[0]()

    def meet(lo, hi):
        return pltpu.roll(jnp.where(left[: lo.shape[-2]], hi, lo), 64, lo.ndim - 1)

    kay[1]()
    for y in range(3):
        rows = slice(8 + 8 * y, 16 + 8 * y)
        for j in range(4):
            lo, hi = RK[0, y, j], RK[1, y, j]
            CK[2 + j, rows, :] = jnp.where(left, lo, hi)
            CK[9 - j, rows, :] = meet(lo, hi)
    two[1]()
    for j in range(4):
        lo, hi = RB[0, :, j], RB[1, :, j]
        CB[:, 2 + j, 16:24, :] = jnp.where(left, lo, hi)
        CB[:, 9 - j, 16:24, :] = meet(lo, hi)
    for y, rows, back1, back0 in ((0, slice(8, 16), 5, 6), (1, slice(24, 32), 3, 2)):
        for part in (0, 1):
            lo, hi = RD[0, y, part], RD[1, y, part]
            CB[:, 9 - 2 * part, rows, :] = meet(lo, hi)
            CB[:, 8 - 2 * part, rows, :] = jnp.where(left, lo, hi)
        odd, even = jnp.where(left, RD[0, y, 2], RD[1, y, 2]), meet(RD[0, y, 2], RD[1, y, 2])
        CB[:, 5, rows, :] = odd
        CB[:, 3, rows, :] = pltpu.roll(odd, back1, 1)
        CB[:, 4, rows, :] = even
        CB[:, 2, rows, :] = pltpu.roll(even, back0, 1)
    for f in range(3):
        CB[f, 1, 16:24, :] = meet(R2[0, f], R2[1, f])
    for y, near, far in ((0, 15, 7), (1, 24, 32)):
        near_row = meet(RN[0, y, 0:3], RN[1, y, 0:3])
        far_row = meet(RM2[0, y, 0:3], RM2[1, y, 0:3])
        for f in range(3):
            CB[f, 1, near : near + 1, :] = near_row[f : f + 1]
            CB[f, 9, far : far + 1, :] = far_row[f : f + 1]
            for j in range(4):
                CB[f, 10 + j, far : far + 1, :] = RY2[y, j, f : f + 1]

    ends_c = lane_ends(64)
    theta_c, steps = rates(0.05, 2.0, COARSE_STEPS)

    def coarse_k_at(x, r0, n):
        return CK[x, r0 : r0 + n, :]

    at = CB
    for t in range(2, COARSE_STEPS + 1):
        a, b = steps[t - 2]
        to = CY if t % 2 == 0 else CX
        if t == 2:
            coefs, prev = ((1.0 + a - b) / theta_c + b, b / theta_c, 0.0, 0.0), None
        elif t == 3:
            coefs, prev = (1.0 + a - b, b, b - a / theta_c, 0.0), None
        else:
            coefs, prev = (1.0 + a - b, b, b, -a), to
        sweep(to, at, prev, CB, coarse_k_at, coefs, range(t, 14), coarse_rows(t), ends_c, 13)
        at = to

    repeat = (
        lax.broadcasted_iota(jnp.int32, (128, 256), 1) // 2 == lax.broadcasted_iota(jnp.int32, (128, 256), 0)
    ).astype(jnp.float32)
    pre[1]()
    pre[2]()
    for x in range(16):
        XC[:, 4 + x, 4:8, :] = RPY[0, :, x]
        XC[:, 4 + x, 24:28, :] = RPY[1, :, x]
    for cx, x0 in ((0, 1), (1, 20)):
        XC[:, x0 : x0 + 3, 4:8, :] = RPC[2 * cx]
        XC[:, x0 : x0 + 3, 24:28, :] = RPC[2 * cx + 1]
    for f in range(3):
        for i in range(6):
            v = at[f, 8 + i, 14:26, :]
            ZF[f, i, pl.ds(0, 12, 2), :] = v
            ZF[f, i, pl.ds(1, 12, 2), :] = v
        up = jnp.dot(
            ZF[f].reshape(144, 128), repeat, precision=lax.Precision.HIGHEST, preferred_element_type=jnp.float32
        ).reshape(6, 24, 256)
        for i in range(6):
            for x, v in ((2 * i, up[i, :, 0:128]), (22 - 2 * i, up[i, :, 128:256])):
                XC[f, x, 4:28, :] = XC[f, x, 4:28, :] + v
                XC[f, x + 1, 4:28, :] = XC[f, x + 1, 4:28, :] + v
    for _, _, drain in (one, kay, two):
        drain()


def after(XC, BK, DG, out_sol, out_rem, XA, XB, RM, out_sem):
    ends = lane_ends(128)
    theta, ((a1, b1), (a2, b2)) = rates(0.5, 2.0, SMOOTH)

    def fine_k(x, r0, n):
        return BK[3, x, r0 : r0 + n, :]

    sweep(XA, XC, None, BK, fine_k, (1.0 - 1.0 / theta, 1.0 / theta, 1.0 / theta, 0.0), range(1, 23), fine_rows(3), ends)
    sweep(XB, XA, XC, BK, fine_k, (1.0 + a1 - b1, b1, b1, -a1), range(2, 22), fine_rows(2), ends)
    sweep(XA, XB, XA, BK, fine_k, (1.0 + a2 - b2, b2, b2, -a2), range(3, 21), fine_rows(1), ends)
    put = [
        pltpu.make_async_copy(XA.at[:, 4:20, 8:24, :], out_sol, out_sem.at[0]),
        pltpu.make_async_copy(RM, out_rem, out_sem.at[1]),
    ]
    put[0].start()
    held = {}
    for x in range(4, 20):
        v, nb = around(XA, x, (8, 16), ends, held)
        RM[:, x - 4] = DG[x - 4][None] * (BK[0:3, x, 8:24, :] - v + fine_k(x, 8, 16)[None] * nb)
    put[1].start()
    put[0].wait()
    put[1].wait()


def local(nx, ny, load, modulus, anchor, wall_mask):
    f32 = jnp.float32

    def vmem(*shape):
        return pltpu.VMEM(shape, f32)

    dma = pltpu.SemaphoreType.DMA
    far = pl.BlockSpec(memory_space=pltpu.HBM)
    near = pl.BlockSpec(memory_space=pltpu.VMEM)
    inner = pl.pallas_call(
        functools.partial(kernel, nx, ny),
        out_shape=(
            jax.ShapeDtypeStruct((3, 24, 32, 128), f32),
            jax.ShapeDtypeStruct((4, 24, 32, 128), f32),
            jax.ShapeDtypeStruct((16, 16, 128), f32),
        ),
        in_specs=[far] * 4,
        out_specs=(near, near, near),
        scratch_shapes=[
            vmem(3, 16, 16, 128), vmem(16, 16, 128), vmem(16, 16, 128),
            pltpu.VMEM((4, 4, 16), jnp.int32), vmem(16, 16, 128), vmem(3, 24, 32, 128),
            vmem(2, 4, 16, 4, 128), vmem(2, 4, 16, 4, 128), vmem(4, 4, 2, 4, 128), vmem(4, 4, 2, 4, 128),
            vmem(2, 3, 16, 4, 128), vmem(2, 3, 16, 4, 128), vmem(4, 3, 3, 4, 128), vmem(4, 3, 3, 4, 128),
            vmem(2, 8, 16, 128), vmem(2, 4, 8, 256), vmem(3, 8, 16, 128), vmem(3, 4, 8, 256),
            vmem(4, 8, 128), vmem(3, 4, 8, 128), vmem(4, 8, 128), vmem(2, 4, 4, 128),
            vmem(3, 14, 40, 128), vmem(14, 40, 128), vmem(3, 14, 40, 128), vmem(3, 14, 40, 128),
            vmem(2, 3, 4, 8, 128), vmem(2, 2, 3, 3, 8, 128), vmem(2, 2, 3, 3, 8, 128),
            vmem(2, 3, 4, 8, 128), vmem(2, 3, 8, 128),
            vmem(2, 4, 4, 128), vmem(2, 2, 4, 128), vmem(2, 2, 4, 128),
            vmem(3, 6, 24, 128),
            dma((4,)), dma((8,)), dma((8,)), dma((8,)), dma((8,)), dma((20,)), dma((20,)), dma((8,)), dma((8,)),
        ],
        compiler_params=pltpu.CompilerParams(collective_id=0, has_side_effects=True, vmem_limit_bytes=24 << 20),
    )(*(pltpu.with_memory_space_constraint(a, pltpu.HBM) for a in (load, modulus, anchor, wall_mask)))
    shape = jax.ShapeDtypeStruct((3, 16, 16, 128), f32)
    return pl.pallas_call(
        after,
        out_shape=(shape, shape),
        in_specs=[near] * 3,
        out_specs=(far, far),
        scratch_shapes=[vmem(3, 24, 32, 128), vmem(3, 24, 32, 128), vmem(3, 16, 16, 128), dma((2,))],
        compiler_params=pltpu.CompilerParams(vmem_limit_bytes=16 << 20),
    )(*inner)


def solution(mesh):
    return jax.shard_map(
        functools.partial(local, mesh.shape["gx"], mesh.shape["gy"]),
        mesh=mesh,
        in_specs=(
            P(None, "gx", "gy", None),
            P("gx", "gy", None),
            P("gx", "gy", None),
            P("gx", "gy", None),
        ),
        out_specs=(P(None, "gx", "gy", None), P(None, "gx", "gy", None)),
        check_vma=False,
    )
```

```python
import functools
import jax
import jax.numpy as jnp
from jax import lax
from jax.experimental import pallas as pl
from jax.experimental.pallas import tpu as pltpu
from jax.sharding import PartitionSpec as P

SMOOTH = 3
COARSE_STEPS = 8
MESH = pl.DeviceIdType.MESH

NEAR = [(-1, -1), (-1, 1), (1, -1), (1, 1), (-1, 0), (1, 0), (0, -1), (0, 1)]
FAR = [(-2, 0), (2, 0), (0, -2), (0, 2)]
KNIGHT = [(s * a, t * b) for a, b in ((2, 1), (1, 2)) for s in (-1, 1) for t in (-1, 1)]
ALL = KNIGHT + FAR + NEAR


def rates(low, high, steps):
    theta, delta = (high + low) / 2.0, (high - low) / 2.0
    sigma = theta / delta
    rho = 1.0 / sigma
    out = []
    for _ in range(steps - 1):
        rho_next = 1.0 / (2.0 * sigma - rho)
        out.append((rho_next * rho, 2.0 * rho_next / delta))
        rho = rho_next
    return theta, out


def around(src, x, rows, ends, held, fold=False):
    r0, n = rows
    first, last = ends[n]

    def plane(p):
        if (p, rows) not in held:
            held[p, rows] = src[0:3, p, r0 : r0 + n, :]
        return held[p, rows]

    below, v = plane(x - 1), plane(x)
    above = pltpu.roll(v, 64, 2) if fold else plane(x + 1)
    nb = jnp.where(first, 0.0, pltpu.roll(v, 1, 2)) + jnp.where(last, 0.0, pltpu.roll(v, 127, 2))
    nb = nb + (below + above)
    nb = nb + (src[0:3, x, r0 - 1 : r0 + n - 1, :] + src[0:3, x, r0 + 1 : r0 + n + 1, :])
    return v, nb


def sweep(dst, src, prev, rhs, stiff, coefs, planes, rows_of, ends, fold_at=None):
    cv, cn, cb, cp = coefs
    held = {}
    for x in planes:
        r0, n = rows_of(x)
        v, nb = around(src, x, (r0, n), ends, held, x == fold_at)
        out = cv * v + (cn * stiff(x, r0, n))[None] * nb
        if cb:
            out = out + cb * rhs[0:3, x, r0 : r0 + n, :]
        if prev is not None:
            out = out + cp * prev[0:3, x, r0 : r0 + n, :]
        dst[0:3, x, r0 : r0 + n, :] = out


def lane_ends(period):
    lane = lax.broadcasted_iota(jnp.int32, (3, 24, 128), 2) % period
    first, last = lane == 0, lane == period - 1
    return {24: (first, last), 16: (first[:, :16], last[:, :16])}


def fine_rows(reach):
    return lambda x: (8, 16) if x in (4 - reach, 19 + reach) else (4, 24)


def coarse_rows(step):
    def of(x):
        away = max(0, 10 - x)
        return (12, 16) if (11 - step - away if away else 10 - step) <= 4 else (8, 24)

    return of


def kernel(
    nx, ny, load, modulus, anchor, wall_mask, XC, BK, DG,
    f_load, f_mod, f_anc, mask, INV, XA, SY, RY, SC, RC, SPY, RPY, SPC, RPC,
    ZC, LC, ZR, LH, IDC, PB, PK, Q, CB, CK, CX, CY, RB, RD, PC, RK, R2, RY2, RN, RM2, ZF,
    in_sem, s1, r1, sk, rk, s2, r2, sp, rp,
):
    ix, iy = lax.axis_index("gx"), lax.axis_index("gy")

    def there(d):
        conds = []
        if d[0] < 0:
            conds.append(ix >= -d[0])
        if d[0] > 0:
            conds.append(ix < nx - d[0])
        if d[1] < 0:
            conds.append(iy >= -d[1])
        if d[1] > 0:
            conds.append(iy < ny - d[1])
        return functools.reduce(jnp.logical_and, conds)

    def device(d):
        return (ix + d[0], iy + d[1])

    def opposite(d):
        return (-d[0], -d[1])

    barrier = pltpu.get_barrier_semaphore()
    for d in NEAR:

        @pl.when(there(d))
        def _():
            pl.semaphore_signal(barrier, inc=1, device_id=device(d), device_id_type=MESH)

    fetch = [
        pltpu.make_async_copy(modulus, f_mod, in_sem.at[0]),
        pltpu.make_async_copy(anchor, f_anc, in_sem.at[1]),
        pltpu.make_async_copy(wall_mask, mask, in_sem.at[2]),
        pltpu.make_async_copy(load, f_load, in_sem.at[3]),
    ]
    for copy in fetch:
        copy.start()

    def lo_hi(s):
        return 0 if s < 0 else 1

    def first_from(d):
        if d[1] == 0:
            return BK.at[:, 1:4, 8:24, :] if d[0] < 0 else BK.at[:, 20:23, 8:24, :]
        if d[0] == 0:
            return RY.at[lo_hi(d[1])]
        return RC.at[2 * lo_hi(d[0]) + lo_hi(d[1])]

    def first_to(d):
        if d[1] == 0:
            return BK.at[:, 4:7, 8:24, :] if d[0] < 0 else BK.at[:, 17:20, 8:24, :]
        if d[0] == 0:
            return SY.at[lo_hi(d[1])]
        return SC.at[2 * lo_hi(d[0]) + lo_hi(d[1])]

    def pre_from(d):
        if d[1] == 0:
            return XC.at[:, 0:3, 8:24, :] if d[0] < 0 else XC.at[:, 21:24, 8:24, :]
        if d[0] == 0:
            return RPY.at[lo_hi(d[1])]
        return RPC.at[2 * lo_hi(d[0]) + lo_hi(d[1])]

    def pre_to(d):
        if d[1] == 0:
            return XC.at[:, 5:8, 8:24, :] if d[0] < 0 else XC.at[:, 16:19, 8:24, :]
        if d[0] == 0:
            return SPY.at[lo_hi(d[1])]
        return SPC.at[2 * lo_hi(d[0]) + lo_hi(d[1])]

    def stiff_from(d):
        if d[0] == 0:
            return CK.at[10:14, 8:16, :] if d[1] < 0 else CK.at[10:14, 24:32, :]
        return RK.at[lo_hi(d[0]), d[1] + 1]

    def stiff_to(d):
        return PK

    def coarse_from(d):
        if abs(d[0]) < 2 and abs(d[1]) < 2:
            if d[0] == 0:
                return CB.at[:, 10:14, 8:16, :] if d[1] < 0 else CB.at[:, 10:14, 24:32, :]
            return RB.at[lo_hi(d[0])] if d[1] == 0 else RD.at[lo_hi(d[0]), lo_hi(d[1])]
        if d[1] == 0:
            return R2.at[lo_hi(d[0])]
        if d[0] == 0:
            return RY2.at[lo_hi(d[1])]
        if abs(d[0]) == 2:
            return RN.at[lo_hi(d[0]), lo_hi(d[1])]
        return RM2.at[lo_hi(d[0]), lo_hi(d[1])]

    def coarse_to(d):
        if abs(d[0]) < 2 and abs(d[1]) < 2:
            return PB if d[0] == 0 or d[1] == 0 else PC.at[lo_hi(d[0]), lo_hi(d[1])]
        if d[1] == 0:
            return PB.at[:, 0]
        if d[0] == 0:
            return Q.at[lo_hi(d[1])]
        return Q.at[lo_hi(d[1]), 0]

    def exchange(partners, to, came, send, recv):
        def copy(k, d):
            return pltpu.make_async_remote_copy(
                src_ref=to(d), dst_ref=came(opposite(d)), send_sem=send.at[k], recv_sem=recv.at[k],
                device_id=device(d), device_id_type=MESH,
            )

        def start():
            for k, d in enumerate(partners):

                @pl.when(there(d))
                def _():
                    copy(k, d).start()

        def wait(chosen=lambda d: True):
            for k, d in enumerate(partners):
                if not chosen(d):
                    continue

                @pl.when(there(opposite(d)))
                def _():
                    copy(k, d).wait_recv()

        def drain():
            for k, d in enumerate(partners):

                @pl.when(there(d))
                def _():
                    copy(k, d).wait_send()

        return start, wait, drain

    one = exchange(NEAR, first_to, first_from, s1, r1)
    pre = exchange(NEAR, pre_to, pre_from, sp, rp)
    kay = exchange(NEAR, stiff_to, stiff_from, sk, rk)
    two = exchange(ALL, coarse_to, coarse_from, s2, r2)

    for partners, came in ((NEAR, first_from), (NEAR, pre_from), (NEAR, stiff_from), (ALL, coarse_from)):
        for d in partners:

            @pl.when(jnp.logical_not(there(d)))
            def _():
                place = came(d)
                place[...] = jnp.zeros(place.shape, jnp.float32)

    spread = (
        lax.broadcasted_iota(jnp.int32, (16, 128), 1) // 8 == lax.broadcasted_iota(jnp.int32, (16, 128), 0)
    ).astype(jnp.float32)
    rows4 = (
        lax.broadcasted_iota(jnp.int32, (16, 4), 0) // 4 == lax.broadcasted_iota(jnp.int32, (16, 4), 1)
    ).astype(jnp.float32)
    fetch[0].wait()
    fetch[1].wait()
    fetch[2].wait()
    for b in range(4):
        wall = jnp.dot(mask[b].astype(jnp.float32), spread, preferred_element_type=jnp.float32)
        wall = jnp.dot(rows4, wall, preferred_element_type=jnp.float32)
        for x in range(4 * b, 4 * b + 4):
            stiff = f_mod[x] * (0.2 + wall)
            diag = f_anc[x] + 6.0 * stiff
            inv = 1.0 / diag
            DG[x] = diag
            INV[x] = inv
            BK[3, 4 + x, 8:24, :] = stiff * inv
            f_mod[x] = stiff
    fetch[3].wait()
    for x in range(16):
        BK[0:3, 4 + x, 8:24, :] = f_load[:, x] * INV[x][None]
    for x in range(16):
        SY[0, :, x] = BK[:, 4 + x, 8:12, :]
        SY[1, :, x] = BK[:, 4 + x, 20:24, :]
    for cx, x0 in ((0, 4), (1, 18)):
        SC[2 * cx] = BK[:, x0 : x0 + 2, 8:12, :]
        SC[2 * cx + 1] = BK[:, x0 : x0 + 2, 20:24, :]

    pl.semaphore_wait(barrier, sum(there(d).astype(jnp.int32) for d in NEAR))
    one[0]()

    pair_sum = 0.125 * (
        lax.broadcasted_iota(jnp.int32, (256, 128), 0) // 2 == lax.broadcasted_iota(jnp.int32, (256, 128), 1)
    ).astype(jnp.float32)

    def gather_pairs(place, lhs, f):
        for c in range(8):
            v = place[f, c, pl.ds(0, 8, 2), :] + place[f, c, pl.ds(1, 8, 2), :]
            if c < 4:
                lhs[f, c, :, 0:128] = v
            else:
                lhs[f, 7 - c, :, 128:256] = v

    def boxes(lhs, count):
        flat = lhs[...].reshape(count * 32, 256)
        return jnp.dot(flat, pair_sum, precision=lax.Precision.HIGHEST, preferred_element_type=jnp.float32)

    for c in range(8):
        ZC[0, c] = f_mod[2 * c] + f_mod[2 * c + 1]
        ZC[1, c] = f_anc[2 * c] + f_anc[2 * c + 1]
    gather_pairs(ZC, LC, 0)
    gather_pairs(ZC, LC, 1)
    means = boxes(LC, 2)
    coarse_stiff = 0.25 * means[0:32]
    inv = 1.0 / (means[32:64] + 6.0 * coarse_stiff)
    IDC[...] = inv.reshape(4, 8, 128)
    coarse_k = (coarse_stiff * inv).reshape(4, 8, 128)
    PK[...] = coarse_k
    CK[10:14, 16:24, :] = coarse_k
    kay[0]()

    ends = lane_ends(128)
    theta, ((a1, b1), (a2, b2)) = rates(0.5, 2.0, SMOOTH)

    def fine_k(x, r0, n):
        return BK[3, x, r0 : r0 + n, :]

    def smooth(second, third, pairs):
        coefs = ((1.0 + a1 - b1) / theta + b1, b1 / theta, 0.0, 0.0)
        for planes in second:
            sweep(XA, BK, None, BK, fine_k, coefs, planes, fine_rows(2), ends)
        coefs = (1.0 + a2 - b2, b2, b2 - a2 / theta, 0.0)
        for planes in third:
            sweep(XC, XA, None, BK, fine_k, coefs, planes, fine_rows(1), ends)
        held = {}
        for c in pairs:
            total = 0.0
            for x in (4 + 2 * c, 5 + 2 * c):
                v, nb = around(XC, x, (8, 16), ends, held)
                total = total + DG[x - 4][None] * (BK[0:3, x, 8:24, :] - v + fine_k(x, 8, 16)[None] * nb)
            ZR[:, c] = total

    one[1](lambda d: d[0] == 0)
    for x in range(16):
        BK[:, 4 + x, 4:8, :] = RY[0, :, x]
        BK[:, 4 + x, 24:28, :] = RY[1, :, x]
    smooth([range(5, 19)], [range(6, 18)], range(2, 6))
    one[1](lambda d: d[0] != 0)
    for cx, x0 in ((0, 2), (1, 20)):
        BK[:, x0 : x0 + 2, 4:8, :] = RC[2 * cx]
        BK[:, x0 : x0 + 2, 24:28, :] = RC[2 * cx + 1]
    smooth([range(2, 5), range(19, 22)], [range(3, 6), range(18, 21)], (0, 1, 6, 7))

    for f in range(3):
        gather_pairs(ZR, LH, f)
    rest = boxes(LH, 3).reshape(3, 4, 8, 128) * IDC[...][None]
    PB[...] = rest
    left = lax.broadcasted_iota(jnp.int32, (8, 128), 1) < 64
    row = lax.broadcasted_iota(jnp.int32, (8, 128), 0)
    for dx in (0, 1):
        far_half = left if dx else jnp.logical_not(left)
        first_two = jnp.where(far_half, pltpu.roll(rest[:, 1], 64, 2), rest[:, 0])
        last_two = jnp.where(far_half, pltpu.roll(rest[:, 3], 64, 2), rest[:, 2])
        for dy, shift1, shift0, has1, has0 in ((0, 5, 6, row >= 5, row >= 6), (1, 3, 2, row < 3, row < 2)):
            odd = jnp.where(has1, pltpu.roll(rest[:, 1], shift1, 1), rest[:, 3])
            even = jnp.where(has0, pltpu.roll(rest[:, 0], shift0, 1), rest[:, 2])
            PC[dx, dy, 0] = first_two
            PC[dx, dy, 1] = last_two
            PC[dx, dy, 2] = jnp.where(far_half, odd, pltpu.roll(even, 64, 2))
    for j in range(4):
        Q[0, j, 0:3] = rest[:, j, 0, :]
        Q[1, j, 0:3] = rest[:, j, 7, :]
    two[0]()
    CB[:, 10:14, 16:24, :] = rest

    for x in range(16):
        SPY[0, :, x] = XC[:, 4 + x, 8:12, :]
        SPY[1, :, x] = XC[:, 4 + x, 20:24, :]
    for cx, x0 in ((0, 4), (1, 17)):
        SPC[2 * cx] = XC[:, x0 : x0 + 3, 8:12, :]
        SPC[2 * cx + 1] = XC[:, x0 : x0 + 3, 20:24, :]
    pre[0]()

    def meet(lo, hi):
        return pltpu.roll(jnp.where(left[: lo.shape[-2]], hi, lo), 64, lo.ndim - 1)

    kay[1]()
    for y in range(3):
        rows = slice(8 + 8 * y, 16 + 8 * y)
        for j in range(4):
            lo, hi = RK[0, y, j], RK[1, y, j]
            CK[2 + j, rows, :] = jnp.where(left, lo, hi)
            CK[9 - j, rows, :] = meet(lo, hi)
    two[1]()
    for j in range(4):
        lo, hi = RB[0, :, j], RB[1, :, j]
        CB[:, 2 + j, 16:24, :] = jnp.where(left, lo, hi)
        CB[:, 9 - j, 16:24, :] = meet(lo, hi)
    for y, rows, back1, back0 in ((0, slice(8, 16), 5, 6), (1, slice(24, 32), 3, 2)):
        for part in (0, 1):
            lo, hi = RD[0, y, part], RD[1, y, part]
            CB[:, 9 - 2 * part, rows, :] = meet(lo, hi)
            CB[:, 8 - 2 * part, rows, :] = jnp.where(left, lo, hi)
        odd, even = jnp.where(left, RD[0, y, 2], RD[1, y, 2]), meet(RD[0, y, 2], RD[1, y, 2])
        CB[:, 5, rows, :] = odd
        CB[:, 3, rows, :] = pltpu.roll(odd, back1, 1)
        CB[:, 4, rows, :] = even
        CB[:, 2, rows, :] = pltpu.roll(even, back0, 1)
    for f in range(3):
        CB[f, 1, 16:24, :] = meet(R2[0, f], R2[1, f])
    for y, near, far in ((0, 15, 7), (1, 24, 32)):
        near_row = meet(RN[0, y, 0:3], RN[1, y, 0:3])
        far_row = meet(RM2[0, y, 0:3], RM2[1, y, 0:3])
        for f in range(3):
            CB[f, 1, near : near + 1, :] = near_row[f : f + 1]
            CB[f, 9, far : far + 1, :] = far_row[f : f + 1]
            for j in range(4):
                CB[f, 10 + j, far : far + 1, :] = RY2[y, j, f : f + 1]

    ends_c = lane_ends(64)
    theta_c, steps = rates(0.05, 2.0, COARSE_STEPS)

    def coarse_k_at(x, r0, n):
        return CK[x, r0 : r0 + n, :]

    at = CB
    for t in range(2, COARSE_STEPS + 1):
        a, b = steps[t - 2]
        to = CY if t % 2 == 0 else CX
        if t == 2:
            coefs, prev = ((1.0 + a - b) / theta_c + b, b / theta_c, 0.0, 0.0), None
        elif t == 3:
            coefs, prev = (1.0 + a - b, b, b - a / theta_c, 0.0), None
        else:
            coefs, prev = (1.0 + a - b, b, b, -a), to
        sweep(to, at, prev, CB, coarse_k_at, coefs, range(t, 14), coarse_rows(t), ends_c, 13)
        at = to

    repeat = (
        lax.broadcasted_iota(jnp.int32, (128, 256), 1) // 2 == lax.broadcasted_iota(jnp.int32, (128, 256), 0)
    ).astype(jnp.float32)
    pre[1]()
    pre[2]()
    for x in range(16):
        XC[:, 4 + x, 4:8, :] = RPY[0, :, x]
        XC[:, 4 + x, 24:28, :] = RPY[1, :, x]
    for cx, x0 in ((0, 1), (1, 20)):
        XC[:, x0 : x0 + 3, 4:8, :] = RPC[2 * cx]
        XC[:, x0 : x0 + 3, 24:28, :] = RPC[2 * cx + 1]
    for f in range(3):
        for i in range(6):
            v = at[f, 8 + i, 14:26, :]
            ZF[f, i, pl.ds(0, 12, 2), :] = v
            ZF[f, i, pl.ds(1, 12, 2), :] = v
        up = jnp.dot(
            ZF[f].reshape(144, 128), repeat, precision=lax.Precision.HIGHEST, preferred_element_type=jnp.float32
        ).reshape(6, 24, 256)
        for i in range(6):
            for x, v in ((2 * i, up[i, :, 0:128]), (22 - 2 * i, up[i, :, 128:256])):
                XC[f, x, 4:28, :] = XC[f, x, 4:28, :] + v
                XC[f, x + 1, 4:28, :] = XC[f, x + 1, 4:28, :] + v
    for _, _, drain in (one, kay, two):
        drain()


def after(XC, BK, DG, out_sol, out_rem, XA, XB, RM, out_sem):
    ends = lane_ends(128)
    theta, ((a1, b1), (a2, b2)) = rates(0.5, 2.0, SMOOTH)

    def fine_k(x, r0, n):
        return BK[3, x, r0 : r0 + n, :]

    sweep(XA, XC, None, BK, fine_k, (1.0 - 1.0 / theta, 1.0 / theta, 1.0 / theta, 0.0), range(1, 23), fine_rows(3), ends)
    sweep(XB, XA, XC, BK, fine_k, (1.0 + a1 - b1, b1, b1, -a1), range(2, 22), fine_rows(2), ends)
    sweep(XA, XB, XA, BK, fine_k, (1.0 + a2 - b2, b2, b2, -a2), range(3, 21), fine_rows(1), ends)
    put = [
        pltpu.make_async_copy(XA.at[:, 4:20, 8:24, :], out_sol, out_sem.at[0]),
        pltpu.make_async_copy(RM, out_rem, out_sem.at[1]),
    ]
    put[0].start()
    held = {}
    for x in range(4, 20):
        v, nb = around(XA, x, (8, 16), ends, held)
        RM[:, x - 4] = DG[x - 4][None] * (BK[0:3, x, 8:24, :] - v + fine_k(x, 8, 16)[None] * nb)
    put[1].start()
    put[0].wait()
    put[1].wait()


def local(nx, ny, load, modulus, anchor, wall_mask):
    f32 = jnp.float32

    def vmem(*shape):
        return pltpu.VMEM(shape, f32)

    dma = pltpu.SemaphoreType.DMA
    far = pl.BlockSpec(memory_space=pltpu.HBM)
    near = pl.BlockSpec(memory_space=pltpu.VMEM)
    inner = pl.pallas_call(
        functools.partial(kernel, nx, ny),
        out_shape=(
            jax.ShapeDtypeStruct((3, 24, 32, 128), f32),
            jax.ShapeDtypeStruct((4, 24, 32, 128), f32),
            jax.ShapeDtypeStruct((16, 16, 128), f32),
        ),
        in_specs=[far] * 4,
        out_specs=(near, near, near),
        scratch_shapes=[
            vmem(3, 16, 16, 128), vmem(16, 16, 128), vmem(16, 16, 128),
            pltpu.VMEM((4, 4, 16), jnp.int32), vmem(16, 16, 128), vmem(3, 24, 32, 128),
            vmem(2, 4, 16, 4, 128), vmem(2, 4, 16, 4, 128), vmem(4, 4, 2, 4, 128), vmem(4, 4, 2, 4, 128),
            vmem(2, 3, 16, 4, 128), vmem(2, 3, 16, 4, 128), vmem(4, 3, 3, 4, 128), vmem(4, 3, 3, 4, 128),
            vmem(2, 8, 16, 128), vmem(2, 4, 8, 256), vmem(3, 8, 16, 128), vmem(3, 4, 8, 256),
            vmem(4, 8, 128), vmem(3, 4, 8, 128), vmem(4, 8, 128), vmem(2, 4, 4, 128),
            vmem(3, 14, 40, 128), vmem(14, 40, 128), vmem(3, 14, 40, 128), vmem(3, 14, 40, 128),
            vmem(2, 3, 4, 8, 128), vmem(2, 2, 3, 3, 8, 128), vmem(2, 2, 3, 3, 8, 128),
            vmem(2, 3, 4, 8, 128), vmem(2, 3, 8, 128),
            vmem(2, 4, 4, 128), vmem(2, 2, 4, 128), vmem(2, 2, 4, 128),
            vmem(3, 6, 24, 128),
            dma((4,)), dma((8,)), dma((8,)), dma((8,)), dma((8,)), dma((20,)), dma((20,)), dma((8,)), dma((8,)),
        ],
        compiler_params=pltpu.CompilerParams(collective_id=0, has_side_effects=True, vmem_limit_bytes=24 << 20),
    )(*(pltpu.with_memory_space_constraint(a, pltpu.HBM) for a in (load, modulus, anchor, wall_mask)))
    shape = jax.ShapeDtypeStruct((3, 16, 16, 128), f32)
    return pl.pallas_call(
        after,
        out_shape=(shape, shape),
        in_specs=[near] * 3,
        out_specs=(far, far),
        scratch_shapes=[vmem(3, 24, 32, 128), vmem(3, 24, 32, 128), vmem(3, 16, 16, 128), dma((2,))],
        compiler_params=pltpu.CompilerParams(vmem_limit_bytes=16 << 20),
    )(*inner)


def solution(mesh):
    return jax.shard_map(
        functools.partial(local, mesh.shape["gx"], mesh.shape["gy"]),
        mesh=mesh,
        in_specs=(
            P(None, "gx", "gy", None),
            P("gx", "gy", None),
            P("gx", "gy", None),
            P("gx", "gy", None),
        ),
        out_specs=(P(None, "gx", "gy", None), P(None, "gx", "gy", None)),
        check_vma=False,
    )
```

```python
import functools
import jax
import jax.numpy as jnp
from jax import lax
from jax.experimental import pallas as pl
from jax.experimental.pallas import tpu as pltpu
from jax.sharding import PartitionSpec as P

SMOOTH = 3
COARSE_STEPS = 8
MESH = pl.DeviceIdType.MESH

NEAR = [(-1, -1), (-1, 1), (1, -1), (1, 1), (-1, 0), (1, 0), (0, -1), (0, 1)]
FAR = [(-2, 0), (2, 0), (0, -2), (0, 2)]
KNIGHT = [(s * a, t * b) for a, b in ((2, 1), (1, 2)) for s in (-1, 1) for t in (-1, 1)]
ALL = KNIGHT + FAR + NEAR[4:6] + NEAR[:4] + NEAR[6:]


def rates(low, high, steps):
    theta, delta = (high + low) / 2.0, (high - low) / 2.0
    sigma = theta / delta
    rho = 1.0 / sigma
    out = []
    for _ in range(steps - 1):
        rho_next = 1.0 / (2.0 * sigma - rho)
        out.append((rho_next * rho, 2.0 * rho_next / delta))
        rho = rho_next
    return theta, out


def around(src, x, rows, ends, held, fold=False):
    r0, n = rows
    first, last = ends[n]

    def plane(p):
        if (p, rows) not in held:
            held[p, rows] = src[0:3, p, r0 : r0 + n, :]
        return held[p, rows]

    below, v = plane(x - 1), plane(x)
    above = pltpu.roll(v, 64, 2) if fold else plane(x + 1)
    nb = jnp.where(first, 0.0, pltpu.roll(v, 1, 2)) + jnp.where(last, 0.0, pltpu.roll(v, 127, 2))
    nb = nb + (below + above)
    nb = nb + (src[0:3, x, r0 - 1 : r0 + n - 1, :] + src[0:3, x, r0 + 1 : r0 + n + 1, :])
    return v, nb


def sweep(dst, src, prev, rhs, stiff, coefs, planes, rows_of, ends, fold_at=None):
    cv, cn, cb, cp = coefs
    held = {}
    for x in planes:
        r0, n = rows_of(x)
        v, nb = around(src, x, (r0, n), ends, held, x == fold_at)
        out = cv * v + (cn * stiff(x, r0, n))[None] * nb
        if cb:
            out = out + cb * rhs[0:3, x, r0 : r0 + n, :]
        if prev is not None:
            out = out + cp * prev[0:3, x, r0 : r0 + n, :]
        dst[0:3, x, r0 : r0 + n, :] = out


def lane_ends(period):
    lane = lax.broadcasted_iota(jnp.int32, (3, 24, 128), 2) % period
    first, last = lane == 0, lane == period - 1
    return {24: (first, last), 16: (first[:, :16], last[:, :16])}


def fine_rows(reach):
    return lambda x: (8, 16) if x in (4 - reach, 19 + reach) else (4, 24)


def coarse_rows(step):
    def of(x):
        away = max(0, 10 - x)
        return (12, 16) if (11 - step - away if away else 10 - step) <= 4 else (8, 24)

    return of


def kernel(
    nx, ny, load, modulus, anchor, wall_mask, XC, BK, DG,
    f_load, f_mod, f_anc, mask, INV, XA, SY, RY, SC, RC, SPY, RPY, SPC, RPC,
    ZC, LC, ZR, LH, IDC, PB, PK, Q, CB, CK, CX, CY, RB, RD, PC, RK, R2, RY2, RN, RM2, ZF,
    in_sem, s1, r1, sk, rk, s2, r2, sp, rp,
):
    ix, iy = lax.axis_index("gx"), lax.axis_index("gy")

    def there(d):
        conds = []
        if d[0] < 0:
            conds.append(ix >= -d[0])
        if d[0] > 0:
            conds.append(ix < nx - d[0])
        if d[1] < 0:
            conds.append(iy >= -d[1])
        if d[1] > 0:
            conds.append(iy < ny - d[1])
        return functools.reduce(jnp.logical_and, conds)

    def device(d):
        return (ix + d[0], iy + d[1])

    def opposite(d):
        return (-d[0], -d[1])

    barrier = pltpu.get_barrier_semaphore()
    for d in NEAR:

        @pl.when(there(d))
        def _():
            pl.semaphore_signal(barrier, inc=1, device_id=device(d), device_id_type=MESH)

    fetch = [
        pltpu.make_async_copy(modulus, f_mod, in_sem.at[0]),
        pltpu.make_async_copy(anchor, f_anc, in_sem.at[1]),
        pltpu.make_async_copy(wall_mask, mask, in_sem.at[2]),
        pltpu.make_async_copy(load, f_load, in_sem.at[3]),
    ]
    for copy in fetch:
        copy.start()

    def lo_hi(s):
        return 0 if s < 0 else 1

    def first_from(d):
        if d[1] == 0:
            return BK.at[:, 1:4, 8:24, :] if d[0] < 0 else BK.at[:, 20:23, 8:24, :]
        if d[0] == 0:
            return RY.at[lo_hi(d[1])]
        return RC.at[2 * lo_hi(d[0]) + lo_hi(d[1])]

    def first_to(d):
        if d[1] == 0:
            return BK.at[:, 4:7, 8:24, :] if d[0] < 0 else BK.at[:, 17:20, 8:24, :]
        if d[0] == 0:
            return SY.at[lo_hi(d[1])]
        return SC.at[2 * lo_hi(d[0]) + lo_hi(d[1])]

    def pre_from(d):
        if d[1] == 0:
            return XC.at[:, 0:3, 8:24, :] if d[0] < 0 else XC.at[:, 21:24, 8:24, :]
        if d[0] == 0:
            return RPY.at[lo_hi(d[1])]
        return RPC.at[2 * lo_hi(d[0]) + lo_hi(d[1])]

    def pre_to(d):
        if d[1] == 0:
            return XC.at[:, 5:8, 8:24, :] if d[0] < 0 else XC.at[:, 16:19, 8:24, :]
        if d[0] == 0:
            return SPY.at[lo_hi(d[1])]
        return SPC.at[2 * lo_hi(d[0]) + lo_hi(d[1])]

    def stiff_from(d):
        if d[0] == 0:
            return CK.at[10:14, 8:16, :] if d[1] < 0 else CK.at[10:14, 24:32, :]
        return RK.at[lo_hi(d[0]), d[1] + 1]

    def stiff_to(d):
        return PK

    def coarse_from(d):
        if abs(d[0]) < 2 and abs(d[1]) < 2:
            if d[0] == 0:
                return CB.at[:, 10:14, 8:16, :] if d[1] < 0 else CB.at[:, 10:14, 24:32, :]
            return RB.at[lo_hi(d[0])] if d[1] == 0 else RD.at[lo_hi(d[0]), lo_hi(d[1])]
        if d[1] == 0:
            return R2.at[lo_hi(d[0])]
        if d[0] == 0:
            return RY2.at[lo_hi(d[1])]
        if abs(d[0]) == 2:
            return RN.at[lo_hi(d[0]), lo_hi(d[1])]
        return RM2.at[lo_hi(d[0]), lo_hi(d[1])]

    def coarse_to(d):
        if abs(d[0]) < 2 and abs(d[1]) < 2:
            return PB if d[0] == 0 or d[1] == 0 else PC.at[lo_hi(d[0]), lo_hi(d[1])]
        if d[1] == 0:
            return PB.at[:, 0]
        if d[0] == 0:
            return Q.at[lo_hi(d[1])]
        return Q.at[lo_hi(d[1]), 0]

    def exchange(partners, to, came, send, recv):
        def copy(k, d):
            return pltpu.make_async_remote_copy(
                src_ref=to(d), dst_ref=came(opposite(d)), send_sem=send.at[k], recv_sem=recv.at[k],
                device_id=device(d), device_id_type=MESH,
            )

        def start():
            for k, d in enumerate(partners):

                @pl.when(there(d))
                def _():
                    copy(k, d).start()

        def wait(chosen=lambda d: True):
            for k, d in enumerate(partners):
                if not chosen(d):
                    continue

                @pl.when(there(opposite(d)))
                def _():
                    copy(k, d).wait_recv()

        def drain():
            for k, d in enumerate(partners):

                @pl.when(there(d))
                def _():
                    copy(k, d).wait_send()

        return start, wait, drain

    one = exchange(NEAR, first_to, first_from, s1, r1)
    pre = exchange(NEAR, pre_to, pre_from, sp, rp)
    kay = exchange(NEAR, stiff_to, stiff_from, sk, rk)
    two = exchange(ALL, coarse_to, coarse_from, s2, r2)

    for partners, came in ((NEAR, first_from), (NEAR, pre_from), (NEAR, stiff_from), (ALL, coarse_from)):
        for d in partners:

            @pl.when(jnp.logical_not(there(d)))
            def _():
                place = came(d)
                place[...] = jnp.zeros(place.shape, jnp.float32)

    spread = (
        lax.broadcasted_iota(jnp.int32, (16, 128), 1) // 8 == lax.broadcasted_iota(jnp.int32, (16, 128), 0)
    ).astype(jnp.float32)
    rows4 = (
        lax.broadcasted_iota(jnp.int32, (16, 4), 0) // 4 == lax.broadcasted_iota(jnp.int32, (16, 4), 1)
    ).astype(jnp.float32)
    fetch[0].wait()
    fetch[1].wait()
    fetch[2].wait()
    for b in range(4):
        wall = jnp.dot(mask[b].astype(jnp.float32), spread, preferred_element_type=jnp.float32)
        wall = jnp.dot(rows4, wall, preferred_element_type=jnp.float32)
        for x in range(4 * b, 4 * b + 4):
            stiff = f_mod[x] * (0.2 + wall)
            diag = f_anc[x] + 6.0 * stiff
            inv = 1.0 / diag
            DG[x] = diag
            INV[x] = inv
            BK[3, 4 + x, 8:24, :] = stiff * inv
            f_mod[x] = stiff
    fetch[3].wait()
    for x in range(16):
        BK[0:3, 4 + x, 8:24, :] = f_load[:, x] * INV[x][None]
    for x in range(16):
        SY[0, :, x] = BK[:, 4 + x, 8:12, :]
        SY[1, :, x] = BK[:, 4 + x, 20:24, :]
    for cx, x0 in ((0, 4), (1, 18)):
        SC[2 * cx] = BK[:, x0 : x0 + 2, 8:12, :]
        SC[2 * cx + 1] = BK[:, x0 : x0 + 2, 20:24, :]

    pl.semaphore_wait(barrier, sum(there(d).astype(jnp.int32) for d in NEAR))
    one[0]()

    pair_sum = 0.125 * (
        lax.broadcasted_iota(jnp.int32, (256, 128), 0) // 2 == lax.broadcasted_iota(jnp.int32, (256, 128), 1)
    ).astype(jnp.float32)

    def gather_pairs(place, lhs, f):
        for c in range(8):
            v = place[f, c, pl.ds(0, 8, 2), :] + place[f, c, pl.ds(1, 8, 2), :]
            if c < 4:
                lhs[f, c, :, 0:128] = v
            else:
                lhs[f, 7 - c, :, 128:256] = v

    def boxes(lhs, count):
        flat = lhs[...].reshape(count * 32, 256)
        return jnp.dot(flat, pair_sum, precision=lax.Precision.HIGHEST, preferred_element_type=jnp.float32)

    for c in range(8):
        ZC[0, c] = f_mod[2 * c] + f_mod[2 * c + 1]
        ZC[1, c] = f_anc[2 * c] + f_anc[2 * c + 1]
    gather_pairs(ZC, LC, 0)
    gather_pairs(ZC, LC, 1)
    means = boxes(LC, 2)
    coarse_stiff = 0.25 * means[0:32]
    inv = 1.0 / (means[32:64] + 6.0 * coarse_stiff)
    IDC[...] = inv.reshape(4, 8, 128)
    coarse_k = (coarse_stiff * inv).reshape(4, 8, 128)
    PK[...] = coarse_k
    CK[10:14, 16:24, :] = coarse_k
    kay[0]()

    ends = lane_ends(128)
    theta, ((a1, b1), (a2, b2)) = rates(0.5, 2.0, SMOOTH)

    def fine_k(x, r0, n):
        return BK[3, x, r0 : r0 + n, :]

    def smooth(second, third, pairs):
        coefs = ((1.0 + a1 - b1) / theta + b1, b1 / theta, 0.0, 0.0)
        for planes in second:
            sweep(XA, BK, None, BK, fine_k, coefs, planes, fine_rows(2), ends)
        coefs = (1.0 + a2 - b2, b2, b2 - a2 / theta, 0.0)
        for planes in third:
            sweep(XC, XA, None, BK, fine_k, coefs, planes, fine_rows(1), ends)
        held = {}
        for c in pairs:
            total = 0.0
            for x in (4 + 2 * c, 5 + 2 * c):
                v, nb = around(XC, x, (8, 16), ends, held)
                total = total + DG[x - 4][None] * (BK[0:3, x, 8:24, :] - v + fine_k(x, 8, 16)[None] * nb)
            ZR[:, c] = total

    one[1](lambda d: d[0] == 0)
    for x in range(16):
        BK[:, 4 + x, 4:8, :] = RY[0, :, x]
        BK[:, 4 + x, 24:28, :] = RY[1, :, x]
    smooth([range(5, 19)], [range(6, 18)], range(2, 6))
    one[1](lambda d: d[0] != 0)
    for cx, x0 in ((0, 2), (1, 20)):
        BK[:, x0 : x0 + 2, 4:8, :] = RC[2 * cx]
        BK[:, x0 : x0 + 2, 24:28, :] = RC[2 * cx + 1]
    smooth([range(2, 5), range(19, 22)], [range(3, 6), range(18, 21)], (0, 1, 6, 7))

    for f in range(3):
        gather_pairs(ZR, LH, f)
    rest = boxes(LH, 3).reshape(3, 4, 8, 128) * IDC[...][None]
    PB[...] = rest
    left = lax.broadcasted_iota(jnp.int32, (8, 128), 1) < 64
    row = lax.broadcasted_iota(jnp.int32, (8, 128), 0)
    for dx in (0, 1):
        far_half = left if dx else jnp.logical_not(left)
        first_two = jnp.where(far_half, pltpu.roll(rest[:, 1], 64, 2), rest[:, 0])
        last_two = jnp.where(far_half, pltpu.roll(rest[:, 3], 64, 2), rest[:, 2])
        for dy, shift1, shift0, has1, has0 in ((0, 5, 6, row >= 5, row >= 6), (1, 3, 2, row < 3, row < 2)):
            odd = jnp.where(has1, pltpu.roll(rest[:, 1], shift1, 1), rest[:, 3])
            even = jnp.where(has0, pltpu.roll(rest[:, 0], shift0, 1), rest[:, 2])
            PC[dx, dy, 0] = first_two
            PC[dx, dy, 1] = last_two
            PC[dx, dy, 2] = jnp.where(far_half, odd, pltpu.roll(even, 64, 2))
    for j in range(4):
        Q[0, j, 0:3] = rest[:, j, 0, :]
        Q[1, j, 0:3] = rest[:, j, 7, :]
    two[0]()
    CB[:, 10:14, 16:24, :] = rest

    for x in range(16):
        SPY[0, :, x] = XC[:, 4 + x, 8:12, :]
        SPY[1, :, x] = XC[:, 4 + x, 20:24, :]
    for cx, x0 in ((0, 4), (1, 17)):
        SPC[2 * cx] = XC[:, x0 : x0 + 3, 8:12, :]
        SPC[2 * cx + 1] = XC[:, x0 : x0 + 3, 20:24, :]
    pre[0]()

    def meet(lo, hi):
        return pltpu.roll(jnp.where(left[: lo.shape[-2]], hi, lo), 64, lo.ndim - 1)

    kay[1]()
    for y in range(3):
        rows = slice(8 + 8 * y, 16 + 8 * y)
        for j in range(4):
            lo, hi = RK[0, y, j], RK[1, y, j]
            CK[2 + j, rows, :] = jnp.where(left, lo, hi)
            CK[9 - j, rows, :] = meet(lo, hi)
    two[1]()
    for j in range(4):
        lo, hi = RB[0, :, j], RB[1, :, j]
        CB[:, 2 + j, 16:24, :] = jnp.where(left, lo, hi)
        CB[:, 9 - j, 16:24, :] = meet(lo, hi)
    for y, rows, back1, back0 in ((0, slice(8, 16), 5, 6), (1, slice(24, 32), 3, 2)):
        for part in (0, 1):
            lo, hi = RD[0, y, part], RD[1, y, part]
            CB[:, 9 - 2 * part, rows, :] = meet(lo, hi)
            CB[:, 8 - 2 * part, rows, :] = jnp.where(left, lo, hi)
        odd, even = jnp.where(left, RD[0, y, 2], RD[1, y, 2]), meet(RD[0, y, 2], RD[1, y, 2])
        CB[:, 5, rows, :] = odd
        CB[:, 3, rows, :] = pltpu.roll(odd, back1, 1)
        CB[:, 4, rows, :] = even
        CB[:, 2, rows, :] = pltpu.roll(even, back0, 1)
    for f in range(3):
        CB[f, 1, 16:24, :] = meet(R2[0, f], R2[1, f])
    for y, near, far in ((0, 15, 7), (1, 24, 32)):
        near_row = meet(RN[0, y, 0:3], RN[1, y, 0:3])
        far_row = meet(RM2[0, y, 0:3], RM2[1, y, 0:3])
        for f in range(3):
            CB[f, 1, near : near + 1, :] = near_row[f : f + 1]
            CB[f, 9, far : far + 1, :] = far_row[f : f + 1]
            for j in range(4):
                CB[f, 10 + j, far : far + 1, :] = RY2[y, j, f : f + 1]

    ends_c = lane_ends(64)
    theta_c, steps = rates(0.05, 2.0, COARSE_STEPS)

    def coarse_k_at(x, r0, n):
        return CK[x, r0 : r0 + n, :]

    at = CB
    for t in range(2, COARSE_STEPS + 1):
        a, b = steps[t - 2]
        to = CY if t % 2 == 0 else CX
        if t == 2:
            coefs, prev = ((1.0 + a - b) / theta_c + b, b / theta_c, 0.0, 0.0), None
        elif t == 3:
            coefs, prev = (1.0 + a - b, b, b - a / theta_c, 0.0), None
        else:
            coefs, prev = (1.0 + a - b, b, b, -a), to
        sweep(to, at, prev, CB, coarse_k_at, coefs, range(t, 14), coarse_rows(t), ends_c, 13)
        at = to

    repeat = (
        lax.broadcasted_iota(jnp.int32, (128, 256), 1) // 2 == lax.broadcasted_iota(jnp.int32, (128, 256), 0)
    ).astype(jnp.bfloat16)
    pre[1]()
    pre[2]()
    for x in range(16):
        XC[:, 4 + x, 4:8, :] = RPY[0, :, x]
        XC[:, 4 + x, 24:28, :] = RPY[1, :, x]
    for cx, x0 in ((0, 1), (1, 20)):
        XC[:, x0 : x0 + 3, 4:8, :] = RPC[2 * cx]
        XC[:, x0 : x0 + 3, 24:28, :] = RPC[2 * cx + 1]
    for f in range(3):
        for i in range(6):
            v = at[f, 8 + i, 14:26, :]
            ZF[f, i, pl.ds(0, 12, 2), :] = v
            ZF[f, i, pl.ds(1, 12, 2), :] = v
        whole = ZF[f].reshape(144, 128)
        up = 0.0
        for _ in range(3):
            piece = whole.astype(jnp.bfloat16)
            up = up + jnp.dot(piece, repeat, preferred_element_type=jnp.float32)
            whole = whole - piece.astype(jnp.float32)
        up = up.reshape(6, 24, 256)
        for i in range(6):
            for x, v in ((2 * i, up[i, :, 0:128]), (22 - 2 * i, up[i, :, 128:256])):
                XC[f, x, 4:28, :] = XC[f, x, 4:28, :] + v
                XC[f, x + 1, 4:28, :] = XC[f, x + 1, 4:28, :] + v
    for _, _, drain in (one, kay, two):
        drain()


def after(XC, BK, DG, out_sol, out_rem, XA, XB, RM, out_sem):
    ends = lane_ends(128)
    theta, ((a1, b1), (a2, b2)) = rates(0.5, 2.0, SMOOTH)

    def fine_k(x, r0, n):
        return BK[3, x, r0 : r0 + n, :]

    sweep(XA, XC, None, BK, fine_k, (1.0 - 1.0 / theta, 1.0 / theta, 1.0 / theta, 0.0), range(1, 23), fine_rows(3), ends)
    sweep(XB, XA, XC, BK, fine_k, (1.0 + a1 - b1, b1, b1, -a1), range(2, 22), fine_rows(2), ends)
    sweep(XA, XB, XA, BK, fine_k, (1.0 + a2 - b2, b2, b2, -a2), range(3, 21), fine_rows(1), ends)
    put = [
        pltpu.make_async_copy(XA.at[:, 4:20, 8:24, :], out_sol, out_sem.at[0]),
        *(
            pltpu.make_async_copy(RM.at[:, a : a + 4], out_rem.at[:, a : a + 4], out_sem.at[1 + a // 4])
            for a in range(0, 16, 4)
        ),
    ]
    put[0].start()
    held = {}
    for x in range(4, 20):
        v, nb = around(XA, x, (8, 16), ends, held)
        RM[:, x - 4] = DG[x - 4][None] * (BK[0:3, x, 8:24, :] - v + fine_k(x, 8, 16)[None] * nb)
        if x % 4 == 3:
            put[x // 4].start()
    for copy in put:
        copy.wait()


def local(nx, ny, load, modulus, anchor, wall_mask):
    f32 = jnp.float32

    def vmem(*shape):
        return pltpu.VMEM(shape, f32)

    dma = pltpu.SemaphoreType.DMA
    far = pl.BlockSpec(memory_space=pltpu.HBM)
    near = pl.BlockSpec(memory_space=pltpu.VMEM)
    inner = pl.pallas_call(
        functools.partial(kernel, nx, ny),
        out_shape=(
            jax.ShapeDtypeStruct((3, 24, 32, 128), f32),
            jax.ShapeDtypeStruct((4, 24, 32, 128), f32),
            jax.ShapeDtypeStruct((16, 16, 128), f32),
        ),
        in_specs=[far] * 4,
        out_specs=(near, near, near),
        scratch_shapes=[
            vmem(3, 16, 16, 128), vmem(16, 16, 128), vmem(16, 16, 128),
            pltpu.VMEM((4, 4, 16), jnp.int32), vmem(16, 16, 128), vmem(3, 24, 32, 128),
            vmem(2, 4, 16, 4, 128), vmem(2, 4, 16, 4, 128), vmem(4, 4, 2, 4, 128), vmem(4, 4, 2, 4, 128),
            vmem(2, 3, 16, 4, 128), vmem(2, 3, 16, 4, 128), vmem(4, 3, 3, 4, 128), vmem(4, 3, 3, 4, 128),
            vmem(2, 8, 16, 128), vmem(2, 4, 8, 256), vmem(3, 8, 16, 128), vmem(3, 4, 8, 256),
            vmem(4, 8, 128), vmem(3, 4, 8, 128), vmem(4, 8, 128), vmem(2, 4, 4, 128),
            vmem(3, 14, 40, 128), vmem(14, 40, 128), vmem(3, 14, 40, 128), vmem(3, 14, 40, 128),
            vmem(2, 3, 4, 8, 128), vmem(2, 2, 3, 3, 8, 128), vmem(2, 2, 3, 3, 8, 128),
            vmem(2, 3, 4, 8, 128), vmem(2, 3, 8, 128),
            vmem(2, 4, 4, 128), vmem(2, 2, 4, 128), vmem(2, 2, 4, 128),
            vmem(3, 6, 24, 128),
            dma((4,)), dma((8,)), dma((8,)), dma((8,)), dma((8,)), dma((20,)), dma((20,)), dma((8,)), dma((8,)),
        ],
        compiler_params=pltpu.CompilerParams(collective_id=0, has_side_effects=True, vmem_limit_bytes=24 << 20),
    )(*(pltpu.with_memory_space_constraint(a, pltpu.HBM) for a in (load, modulus, anchor, wall_mask)))
    shape = jax.ShapeDtypeStruct((3, 16, 16, 128), f32)
    return pl.pallas_call(
        after,
        out_shape=(shape, shape),
        in_specs=[near] * 3,
        out_specs=(far, far),
        scratch_shapes=[vmem(3, 24, 32, 128), vmem(3, 24, 32, 128), vmem(3, 16, 16, 128), dma((5,))],
        compiler_params=pltpu.CompilerParams(vmem_limit_bytes=16 << 20),
    )(*inner)


def solution(mesh):
    return jax.shard_map(
        functools.partial(local, mesh.shape["gx"], mesh.shape["gy"]),
        mesh=mesh,
        in_specs=(
            P(None, "gx", "gy", None),
            P("gx", "gy", None),
            P("gx", "gy", None),
            P("gx", "gy", None),
        ),
        out_specs=(P(None, "gx", "gy", None), P(None, "gx", "gy", None)),
        check_vma=False,
    )
```

```python
import functools
import jax
import jax.numpy as jnp
from jax import lax
from jax.experimental import pallas as pl
from jax.experimental.pallas import tpu as pltpu
from jax.sharding import PartitionSpec as P

SMOOTH = 3
COARSE_STEPS = 8
MESH = pl.DeviceIdType.MESH

NEAR = [(-1, -1), (-1, 1), (1, -1), (1, 1), (-1, 0), (1, 0), (0, -1), (0, 1)]
FAR = [(-2, 0), (2, 0), (0, -2), (0, 2)]
KNIGHT = [(s * a, t * b) for a, b in ((2, 1), (1, 2)) for s in (-1, 1) for t in (-1, 1)]
ALL = KNIGHT + FAR + NEAR[4:6] + NEAR[:4] + NEAR[6:]


def rates(low, high, steps):
    theta, delta = (high + low) / 2.0, (high - low) / 2.0
    sigma = theta / delta
    rho = 1.0 / sigma
    out = []
    for _ in range(steps - 1):
        rho_next = 1.0 / (2.0 * sigma - rho)
        out.append((rho_next * rho, 2.0 * rho_next / delta))
        rho = rho_next
    return theta, out


def around(src, x, rows, ends, held, fold=False):
    r0, n = rows
    first, last = ends[n]

    def plane(p):
        if (p, rows) not in held:
            held[p, rows] = src[0:3, p, r0 : r0 + n, :]
        return held[p, rows]

    below, v = plane(x - 1), plane(x)
    above = pltpu.roll(v, 64, 2) if fold else plane(x + 1)
    nb = jnp.where(first, 0.0, pltpu.roll(v, 1, 2)) + jnp.where(last, 0.0, pltpu.roll(v, 127, 2))
    nb = nb + (below + above)
    nb = nb + (src[0:3, x, r0 - 1 : r0 + n - 1, :] + src[0:3, x, r0 + 1 : r0 + n + 1, :])
    return v, nb


def sweep(dst, src, prev, rhs, stiff, coefs, planes, rows_of, ends, fold_at=None):
    cv, cn, cb, cp = coefs
    held = {}
    for x in planes:
        r0, n = rows_of(x)
        v, nb = around(src, x, (r0, n), ends, held, x == fold_at)
        out = cv * v + (cn * stiff(x, r0, n))[None] * nb
        if cb:
            out = out + cb * rhs[0:3, x, r0 : r0 + n, :]
        if prev is not None:
            out = out + cp * prev[0:3, x, r0 : r0 + n, :]
        dst[0:3, x, r0 : r0 + n, :] = out


def lane_ends(period):
    lane = lax.broadcasted_iota(jnp.int32, (3, 24, 128), 2) % period
    first, last = lane == 0, lane == period - 1
    return {24: (first, last), 16: (first[:, :16], last[:, :16])}


def fine_rows(reach):
    return lambda x: (8, 16) if x in (4 - reach, 19 + reach) else (4, 24)


def coarse_rows(step):
    def of(x):
        away = max(0, 10 - x)
        return (12, 16) if (11 - step - away if away else 10 - step) <= 4 else (8, 24)

    return of


def kernel(
    nx, ny, load, modulus, anchor, wall_mask, XC, BK, DG,
    f_load, f_mod, f_anc, mask, INV, XA, SY, RY, SC, RC, SPY, RPY, SPC, RPC,
    ZC, LC, ZR, LH, IDC, PB, PK, Q, CB, CK, CX, CY, RB, RD, PC, RK, R2, RY2, RN, RM2, ZF,
    in_sem, s1, r1, sk, rk, s2, r2, sp, rp, s3, r3,
):
    ix, iy = lax.axis_index("gx"), lax.axis_index("gy")

    def there(d):
        conds = []
        if d[0] < 0:
            conds.append(ix >= -d[0])
        if d[0] > 0:
            conds.append(ix < nx - d[0])
        if d[1] < 0:
            conds.append(iy >= -d[1])
        if d[1] > 0:
            conds.append(iy < ny - d[1])
        return functools.reduce(jnp.logical_and, conds)

    def device(d):
        return (ix + d[0], iy + d[1])

    def opposite(d):
        return (-d[0], -d[1])

    barrier = pltpu.get_barrier_semaphore()
    for d in NEAR:

        @pl.when(there(d))
        def _():
            pl.semaphore_signal(barrier, inc=1, device_id=device(d), device_id_type=MESH)

    fetch = [
        pltpu.make_async_copy(modulus, f_mod, in_sem.at[0]),
        pltpu.make_async_copy(anchor, f_anc, in_sem.at[1]),
        pltpu.make_async_copy(wall_mask, mask, in_sem.at[2]),
        pltpu.make_async_copy(load, f_load, in_sem.at[3]),
    ]
    for copy in fetch:
        copy.start()

    def lo_hi(s):
        return 0 if s < 0 else 1

    def first_from(d):
        if d[1] == 0:
            return BK.at[:, 1:4, 8:24, :] if d[0] < 0 else BK.at[:, 20:23, 8:24, :]
        if d[0] == 0:
            return RY.at[lo_hi(d[1])]
        return RC.at[2 * lo_hi(d[0]) + lo_hi(d[1])]

    def first_to(d):
        if d[1] == 0:
            return BK.at[:, 4:7, 8:24, :] if d[0] < 0 else BK.at[:, 17:20, 8:24, :]
        if d[0] == 0:
            return SY.at[lo_hi(d[1])]
        return SC.at[2 * lo_hi(d[0]) + lo_hi(d[1])]

    def pre_from(d):
        if d[1] == 0:
            return XC.at[:, 0:3, 8:24, :] if d[0] < 0 else XC.at[:, 21:24, 8:24, :]
        if d[0] == 0:
            return RPY.at[lo_hi(d[1])]
        return RPC.at[2 * lo_hi(d[0]) + lo_hi(d[1])]

    def pre_to(d):
        if d[1] == 0:
            return XC.at[:, 5:8, 8:24, :] if d[0] < 0 else XC.at[:, 16:19, 8:24, :]
        if d[0] == 0:
            return SPY.at[lo_hi(d[1])]
        return SPC.at[2 * lo_hi(d[0]) + lo_hi(d[1])]

    def stiff_from(d):
        if d[0] == 0:
            return CK.at[10:14, 8:16, :] if d[1] < 0 else CK.at[10:14, 24:32, :]
        return RK.at[lo_hi(d[0]), d[1] + 1]

    def stiff_to(d):
        return PK

    def coarse_from(d):
        if abs(d[0]) < 2 and abs(d[1]) < 2:
            if d[0] == 0:
                return CB.at[:, 10:14, 8:16, :] if d[1] < 0 else CB.at[:, 10:14, 24:32, :]
            return RB.at[lo_hi(d[0])] if d[1] == 0 else RD.at[lo_hi(d[0]), lo_hi(d[1]), 0:2]
        if d[1] == 0:
            return R2.at[lo_hi(d[0])]
        if d[0] == 0:
            return RY2.at[lo_hi(d[1])]
        if abs(d[0]) == 2:
            return RN.at[lo_hi(d[0]), lo_hi(d[1])]
        return RM2.at[lo_hi(d[0]), lo_hi(d[1])]

    def coarse_to(d):
        if abs(d[0]) < 2 and abs(d[1]) < 2:
            return PB if d[0] == 0 or d[1] == 0 else PC.at[lo_hi(d[0]), lo_hi(d[1]), 0:2]
        if d[1] == 0:
            return PB.at[:, 0]
        if d[0] == 0:
            return Q.at[lo_hi(d[1])]
        return Q.at[lo_hi(d[1]), 0]

    def early_from(d):
        return RD.at[lo_hi(d[0]), lo_hi(d[1]), 2]

    def early_to(d):
        return PC.at[lo_hi(d[0]), lo_hi(d[1]), 2]

    def exchange(partners, to, came, send, recv):
        def copy(k, d):
            return pltpu.make_async_remote_copy(
                src_ref=to(d), dst_ref=came(opposite(d)), send_sem=send.at[k], recv_sem=recv.at[k],
                device_id=device(d), device_id_type=MESH,
            )

        def start():
            for k, d in enumerate(partners):

                @pl.when(there(d))
                def _():
                    copy(k, d).start()

        def wait(chosen=lambda d: True):
            for k, d in enumerate(partners):
                if not chosen(d):
                    continue

                @pl.when(there(opposite(d)))
                def _():
                    copy(k, d).wait_recv()

        def drain():
            for k, d in enumerate(partners):

                @pl.when(there(d))
                def _():
                    copy(k, d).wait_send()

        return start, wait, drain

    one = exchange(NEAR, first_to, first_from, s1, r1)
    pre = exchange(NEAR, pre_to, pre_from, sp, rp)
    kay = exchange(NEAR, stiff_to, stiff_from, sk, rk)
    two = exchange(ALL, coarse_to, coarse_from, s2, r2)
    early = exchange(NEAR[:4], early_to, early_from, s3, r3)

    for partners, came in ((NEAR, first_from), (NEAR, pre_from), (NEAR, stiff_from), (ALL, coarse_from), (NEAR[:4], early_from)):
        for d in partners:

            @pl.when(jnp.logical_not(there(d)))
            def _():
                place = came(d)
                place[...] = jnp.zeros(place.shape, jnp.float32)

    spread = (
        lax.broadcasted_iota(jnp.int32, (16, 128), 1) // 8 == lax.broadcasted_iota(jnp.int32, (16, 128), 0)
    ).astype(jnp.float32)
    rows4 = (
        lax.broadcasted_iota(jnp.int32, (16, 4), 0) // 4 == lax.broadcasted_iota(jnp.int32, (16, 4), 1)
    ).astype(jnp.float32)
    fetch[0].wait()
    fetch[1].wait()
    fetch[2].wait()
    for b in range(4):
        wall = jnp.dot(mask[b].astype(jnp.float32), spread, preferred_element_type=jnp.float32)
        wall = jnp.dot(rows4, wall, preferred_element_type=jnp.float32)
        for x in range(4 * b, 4 * b + 4):
            stiff = f_mod[x] * (0.2 + wall)
            diag = f_anc[x] + 6.0 * stiff
            inv = 1.0 / diag
            DG[x] = diag
            INV[x] = inv
            BK[3, 4 + x, 8:24, :] = stiff * inv
            f_mod[x] = stiff
    fetch[3].wait()
    for x in range(16):
        BK[0:3, 4 + x, 8:24, :] = f_load[:, x] * INV[x][None]
    for x in range(16):
        SY[0, :, x] = BK[:, 4 + x, 8:12, :]
        SY[1, :, x] = BK[:, 4 + x, 20:24, :]
    for cx, x0 in ((0, 4), (1, 18)):
        SC[2 * cx] = BK[:, x0 : x0 + 2, 8:12, :]
        SC[2 * cx + 1] = BK[:, x0 : x0 + 2, 20:24, :]

    pl.semaphore_wait(barrier, sum(there(d).astype(jnp.int32) for d in NEAR))
    one[0]()

    pair_sum = 0.125 * (
        lax.broadcasted_iota(jnp.int32, (256, 128), 0) // 2 == lax.broadcasted_iota(jnp.int32, (256, 128), 1)
    ).astype(jnp.float32)

    def gather_pairs(place, lhs, f, cells=range(8)):
        for c in cells:
            v = place[f, c, pl.ds(0, 8, 2), :] + place[f, c, pl.ds(1, 8, 2), :]
            if c < 4:
                lhs[f, c, :, 0:128] = v
            else:
                lhs[f, 7 - c, :, 128:256] = v

    def boxes(lhs):
        flat = lhs.reshape(-1, 256)
        return jnp.dot(flat, pair_sum, precision=lax.Precision.HIGHEST, preferred_element_type=jnp.float32)

    for c in range(8):
        ZC[0, c] = f_mod[2 * c] + f_mod[2 * c + 1]
        ZC[1, c] = f_anc[2 * c] + f_anc[2 * c + 1]
    gather_pairs(ZC, LC, 0)
    gather_pairs(ZC, LC, 1)
    means = boxes(LC[...])
    coarse_stiff = 0.25 * means[0:32]
    inv = 1.0 / (means[32:64] + 6.0 * coarse_stiff)
    IDC[...] = inv.reshape(4, 8, 128)
    coarse_k = (coarse_stiff * inv).reshape(4, 8, 128)
    PK[...] = coarse_k
    CK[10:14, 16:24, :] = coarse_k
    kay[0]()

    ends = lane_ends(128)
    theta, ((a1, b1), (a2, b2)) = rates(0.5, 2.0, SMOOTH)

    def fine_k(x, r0, n):
        return BK[3, x, r0 : r0 + n, :]

    def smooth(second, third, pairs):
        coefs = ((1.0 + a1 - b1) / theta + b1, b1 / theta, 0.0, 0.0)
        for planes in second:
            sweep(XA, BK, None, BK, fine_k, coefs, planes, fine_rows(2), ends)
        coefs = (1.0 + a2 - b2, b2, b2 - a2 / theta, 0.0)
        for planes in third:
            sweep(XC, XA, None, BK, fine_k, coefs, planes, fine_rows(1), ends)
        held = {}
        for c in pairs:
            total = 0.0
            for x in (4 + 2 * c, 5 + 2 * c):
                v, nb = around(XC, x, (8, 16), ends, held)
                total = total + DG[x - 4][None] * (BK[0:3, x, 8:24, :] - v + fine_k(x, 8, 16)[None] * nb)
            ZR[:, c] = total

    one[1](lambda d: d[0] == 0)
    for x in range(16):
        BK[:, 4 + x, 4:8, :] = RY[0, :, x]
        BK[:, 4 + x, 24:28, :] = RY[1, :, x]
    smooth([range(5, 19)], [range(6, 18)], range(2, 6))
    left = lax.broadcasted_iota(jnp.int32, (8, 128), 1) < 64
    row = lax.broadcasted_iota(jnp.int32, (8, 128), 0)
    for f in range(3):
        gather_pairs(ZR, LH, f, range(2, 6))
    inner = boxes(LH[:, 2:4]).reshape(3, 2, 8, 128) * IDC[2:4][None]
    PB[:, 2:4] = inner
    for dx in (0, 1):
        far_half = left if dx else jnp.logical_not(left)
        for dy in (0, 1):
            PC[dx, dy, 2] = jnp.where(far_half, pltpu.roll(inner[:, 1], 64, 2), inner[:, 0])
    early[0]()
    one[1](lambda d: d[0] != 0)
    for cx, x0 in ((0, 2), (1, 20)):
        BK[:, x0 : x0 + 2, 4:8, :] = RC[2 * cx]
        BK[:, x0 : x0 + 2, 24:28, :] = RC[2 * cx + 1]
    smooth([range(2, 5), range(19, 22)], [range(3, 6), range(18, 21)], (0, 1, 6, 7))

    for f in range(3):
        gather_pairs(ZR, LH, f, (0, 1, 6, 7))
    outer = boxes(LH[:, 0:2]).reshape(3, 2, 8, 128) * IDC[0:2][None]
    PB[:, 0:2] = outer
    rest = [outer[:, 0], outer[:, 1], inner[:, 0], inner[:, 1]]
    for dx in (0, 1):
        far_half = left if dx else jnp.logical_not(left)
        first_two = jnp.where(far_half, pltpu.roll(rest[1], 64, 2), rest[0])
        for dy, shift1, shift0, has1, has0 in ((0, 5, 6, row >= 5, row >= 6), (1, 3, 2, row < 3, row < 2)):
            odd = jnp.where(has1, pltpu.roll(rest[1], shift1, 1), rest[3])
            even = jnp.where(has0, pltpu.roll(rest[0], shift0, 1), rest[2])
            PC[dx, dy, 0] = first_two
            PC[dx, dy, 1] = jnp.where(far_half, odd, pltpu.roll(even, 64, 2))
    for j in range(4):
        Q[0, j, 0:3] = rest[j][:, 0, :]
        Q[1, j, 0:3] = rest[j][:, 7, :]
    two[0]()
    CB[:, 10:14, 16:24, :] = PB[...]

    for x in range(16):
        SPY[0, :, x] = XC[:, 4 + x, 8:12, :]
        SPY[1, :, x] = XC[:, 4 + x, 20:24, :]
    for cx, x0 in ((0, 4), (1, 17)):
        SPC[2 * cx] = XC[:, x0 : x0 + 3, 8:12, :]
        SPC[2 * cx + 1] = XC[:, x0 : x0 + 3, 20:24, :]
    pre[0]()

    def meet(lo, hi):
        return pltpu.roll(jnp.where(left[: lo.shape[-2]], hi, lo), 64, lo.ndim - 1)

    kay[1]()
    for y in range(3):
        rows = slice(8 + 8 * y, 16 + 8 * y)
        for j in range(4):
            lo, hi = RK[0, y, j], RK[1, y, j]
            CK[2 + j, rows, :] = jnp.where(left, lo, hi)
            CK[9 - j, rows, :] = meet(lo, hi)
    early[1]()
    two[1]()
    for j in range(4):
        lo, hi = RB[0, :, j], RB[1, :, j]
        CB[:, 2 + j, 16:24, :] = jnp.where(left, lo, hi)
        CB[:, 9 - j, 16:24, :] = meet(lo, hi)
    for y, rows, back1, back0 in ((0, slice(8, 16), 5, 6), (1, slice(24, 32), 3, 2)):
        for part in (0, 1):
            lo, hi = RD[0, y, 2 * part], RD[1, y, 2 * part]
            CB[:, 9 - 2 * part, rows, :] = meet(lo, hi)
            CB[:, 8 - 2 * part, rows, :] = jnp.where(left, lo, hi)
        odd, even = jnp.where(left, RD[0, y, 1], RD[1, y, 1]), meet(RD[0, y, 1], RD[1, y, 1])
        CB[:, 5, rows, :] = odd
        CB[:, 3, rows, :] = pltpu.roll(odd, back1, 1)
        CB[:, 4, rows, :] = even
        CB[:, 2, rows, :] = pltpu.roll(even, back0, 1)
    for f in range(3):
        CB[f, 1, 16:24, :] = meet(R2[0, f], R2[1, f])
    for y, near, far in ((0, 15, 7), (1, 24, 32)):
        near_row = meet(RN[0, y, 0:3], RN[1, y, 0:3])
        far_row = meet(RM2[0, y, 0:3], RM2[1, y, 0:3])
        for f in range(3):
            CB[f, 1, near : near + 1, :] = near_row[f : f + 1]
            CB[f, 9, far : far + 1, :] = far_row[f : f + 1]
            for j in range(4):
                CB[f, 10 + j, far : far + 1, :] = RY2[y, j, f : f + 1]

    ends_c = lane_ends(64)
    theta_c, steps = rates(0.05, 2.0, COARSE_STEPS)

    def coarse_k_at(x, r0, n):
        return CK[x, r0 : r0 + n, :]

    at = CB
    for t in range(2, COARSE_STEPS + 1):
        a, b = steps[t - 2]
        to = CY if t % 2 == 0 else CX
        if t == 2:
            coefs, prev = ((1.0 + a - b) / theta_c + b, b / theta_c, 0.0, 0.0), None
        elif t == 3:
            coefs, prev = (1.0 + a - b, b, b - a / theta_c, 0.0), None
        else:
            coefs, prev = (1.0 + a - b, b, b, -a), to
        sweep(to, at, prev, CB, coarse_k_at, coefs, range(t, 14), coarse_rows(t), ends_c, 13)
        at = to

    repeat = (
        lax.broadcasted_iota(jnp.int32, (128, 256), 1) // 2 == lax.broadcasted_iota(jnp.int32, (128, 256), 0)
    ).astype(jnp.bfloat16)
    pre[1]()
    pre[2]()
    for x in range(16):
        XC[:, 4 + x, 4:8, :] = RPY[0, :, x]
        XC[:, 4 + x, 24:28, :] = RPY[1, :, x]
    for cx, x0 in ((0, 1), (1, 20)):
        XC[:, x0 : x0 + 3, 4:8, :] = RPC[2 * cx]
        XC[:, x0 : x0 + 3, 24:28, :] = RPC[2 * cx + 1]
    for f in range(3):
        for i in range(6):
            v = at[f, 8 + i, 14:26, :]
            ZF[f, i, pl.ds(0, 12, 2), :] = v
            ZF[f, i, pl.ds(1, 12, 2), :] = v
        whole = ZF[f].reshape(144, 128)
        up = 0.0
        for _ in range(3):
            piece = whole.astype(jnp.bfloat16)
            up = up + jnp.dot(piece, repeat, preferred_element_type=jnp.float32)
            whole = whole - piece.astype(jnp.float32)
        up = up.reshape(6, 24, 256)
        for i in range(6):
            for x, v in ((2 * i, up[i, :, 0:128]), (22 - 2 * i, up[i, :, 128:256])):
                XC[f, x, 4:28, :] = XC[f, x, 4:28, :] + v
                XC[f, x + 1, 4:28, :] = XC[f, x + 1, 4:28, :] + v
    for _, _, drain in (one, kay, early, two):
        drain()


def after(XC, BK, DG, out_sol, out_rem, XA, XB, RM, out_sem):
    ends = lane_ends(128)
    theta, ((a1, b1), (a2, b2)) = rates(0.5, 2.0, SMOOTH)

    def fine_k(x, r0, n):
        return BK[3, x, r0 : r0 + n, :]

    sweep(XA, XC, None, BK, fine_k, (1.0 - 1.0 / theta, 1.0 / theta, 1.0 / theta, 0.0), range(1, 23), fine_rows(3), ends)
    sweep(XB, XA, XC, BK, fine_k, (1.0 + a1 - b1, b1, b1, -a1), range(2, 22), fine_rows(2), ends)
    sweep(XA, XB, XA, BK, fine_k, (1.0 + a2 - b2, b2, b2, -a2), range(3, 21), fine_rows(1), ends)
    put = [
        pltpu.make_async_copy(XA.at[:, 4:20, 8:24, :], out_sol, out_sem.at[0]),
        *(
            pltpu.make_async_copy(RM.at[:, a : a + 4], out_rem.at[:, a : a + 4], out_sem.at[1 + a // 4])
            for a in range(0, 16, 4)
        ),
    ]
    put[0].start()
    held = {}
    for x in range(4, 20):
        v, nb = around(XA, x, (8, 16), ends, held)
        RM[:, x - 4] = DG[x - 4][None] * (BK[0:3, x, 8:24, :] - v + fine_k(x, 8, 16)[None] * nb)
        if x % 4 == 3:
            put[x // 4].start()
    for copy in put:
        copy.wait()


def local(nx, ny, load, modulus, anchor, wall_mask):
    f32 = jnp.float32

    def vmem(*shape):
        return pltpu.VMEM(shape, f32)

    dma = pltpu.SemaphoreType.DMA
    far = pl.BlockSpec(memory_space=pltpu.HBM)
    near = pl.BlockSpec(memory_space=pltpu.VMEM)
    inner = pl.pallas_call(
        functools.partial(kernel, nx, ny),
        out_shape=(
            jax.ShapeDtypeStruct((3, 24, 32, 128), f32),
            jax.ShapeDtypeStruct((4, 24, 32, 128), f32),
            jax.ShapeDtypeStruct((16, 16, 128), f32),
        ),
        in_specs=[far] * 4,
        out_specs=(near, near, near),
        scratch_shapes=[
            vmem(3, 16, 16, 128), vmem(16, 16, 128), vmem(16, 16, 128),
            pltpu.VMEM((4, 4, 16), jnp.int32), vmem(16, 16, 128), vmem(3, 24, 32, 128),
            vmem(2, 4, 16, 4, 128), vmem(2, 4, 16, 4, 128), vmem(4, 4, 2, 4, 128), vmem(4, 4, 2, 4, 128),
            vmem(2, 3, 16, 4, 128), vmem(2, 3, 16, 4, 128), vmem(4, 3, 3, 4, 128), vmem(4, 3, 3, 4, 128),
            vmem(2, 8, 16, 128), vmem(2, 4, 8, 256), vmem(3, 8, 16, 128), vmem(3, 4, 8, 256),
            vmem(4, 8, 128), vmem(3, 4, 8, 128), vmem(4, 8, 128), vmem(2, 4, 4, 128),
            vmem(3, 14, 40, 128), vmem(14, 40, 128), vmem(3, 14, 40, 128), vmem(3, 14, 40, 128),
            vmem(2, 3, 4, 8, 128), vmem(2, 2, 3, 3, 8, 128), vmem(2, 2, 3, 3, 8, 128),
            vmem(2, 3, 4, 8, 128), vmem(2, 3, 8, 128),
            vmem(2, 4, 4, 128), vmem(2, 2, 4, 128), vmem(2, 2, 4, 128),
            vmem(3, 6, 24, 128),
            dma((4,)), dma((8,)), dma((8,)), dma((8,)), dma((8,)), dma((20,)), dma((20,)), dma((8,)), dma((8,)), dma((4,)), dma((4,)),
        ],
        compiler_params=pltpu.CompilerParams(collective_id=0, has_side_effects=True, vmem_limit_bytes=24 << 20),
    )(*(pltpu.with_memory_space_constraint(a, pltpu.HBM) for a in (load, modulus, anchor, wall_mask)))
    shape = jax.ShapeDtypeStruct((3, 16, 16, 128), f32)
    return pl.pallas_call(
        after,
        out_shape=(shape, shape),
        in_specs=[near] * 3,
        out_specs=(far, far),
        scratch_shapes=[vmem(3, 24, 32, 128), vmem(3, 24, 32, 128), vmem(3, 16, 16, 128), dma((5,))],
        compiler_params=pltpu.CompilerParams(vmem_limit_bytes=16 << 20),
    )(*inner)


def solution(mesh):
    return jax.shard_map(
        functools.partial(local, mesh.shape["gx"], mesh.shape["gy"]),
        mesh=mesh,
        in_specs=(
            P(None, "gx", "gy", None),
            P("gx", "gy", None),
            P("gx", "gy", None),
            P("gx", "gy", None),
        ),
        out_specs=(P(None, "gx", "gy", None), P(None, "gx", "gy", None)),
        check_vma=False,
    )
```

```python
import functools
import jax
import jax.numpy as jnp
from jax import lax
from jax.experimental import pallas as pl
from jax.experimental.pallas import tpu as pltpu
from jax.sharding import PartitionSpec as P

SMOOTH = 3
COARSE_STEPS = 8
MESH = pl.DeviceIdType.MESH

NEAR = [(-1, -1), (-1, 1), (1, -1), (1, 1), (-1, 0), (1, 0), (0, -1), (0, 1)]
FAR = [(-2, 0), (2, 0), (0, -2), (0, 2)]
KNIGHT = [(s * a, t * b) for a, b in ((2, 1), (1, 2)) for s in (-1, 1) for t in (-1, 1)]
ALL = KNIGHT + FAR + NEAR[4:6] + NEAR[:4] + NEAR[6:]


def rates(low, high, steps):
    theta, delta = (high + low) / 2.0, (high - low) / 2.0
    sigma = theta / delta
    rho = 1.0 / sigma
    out = []
    for _ in range(steps - 1):
        rho_next = 1.0 / (2.0 * sigma - rho)
        out.append((rho_next * rho, 2.0 * rho_next / delta))
        rho = rho_next
    return theta, out


def around(src, x, rows, ends, held, fold=False):
    r0, n = rows
    first, last = ends[n]

    def plane(p):
        if (p, rows) not in held:
            held[p, rows] = src[0:3, p, r0 : r0 + n, :]
        return held[p, rows]

    below, v = plane(x - 1), plane(x)
    above = pltpu.roll(v, 64, 2) if fold else plane(x + 1)
    nb = jnp.where(first, 0.0, pltpu.roll(v, 1, 2)) + jnp.where(last, 0.0, pltpu.roll(v, 127, 2))
    nb = nb + (below + above)
    nb = nb + (src[0:3, x, r0 - 1 : r0 + n - 1, :] + src[0:3, x, r0 + 1 : r0 + n + 1, :])
    return v, nb


def sweep(dst, src, prev, rhs, stiff, coefs, planes, rows_of, ends, fold_at=None):
    cv, cn, cb, cp = coefs
    held = {}
    for x in planes:
        r0, n = rows_of(x)
        v, nb = around(src, x, (r0, n), ends, held, x == fold_at)
        if cn == cb:
            out = cv * v + cb * (rhs[0:3, x, r0 : r0 + n, :] + stiff(x, r0, n)[None] * nb)
        else:
            out = cv * v + (cn * stiff(x, r0, n))[None] * nb
            if cb:
                out = out + cb * rhs[0:3, x, r0 : r0 + n, :]
        if prev is not None:
            out = out + cp * prev[0:3, x, r0 : r0 + n, :]
        dst[0:3, x, r0 : r0 + n, :] = out


def lane_ends(period):
    lane = lax.broadcasted_iota(jnp.int32, (3, 24, 128), 2) % period
    first, last = lane == 0, lane == period - 1
    return {24: (first, last), 16: (first[:, :16], last[:, :16])}


def fine_rows(reach):
    return lambda x: (8, 16) if x in (4 - reach, 19 + reach) else (4, 24)


def coarse_rows(step):
    def of(x):
        away = max(0, 10 - x)
        return (12, 16) if (11 - step - away if away else 10 - step) <= 4 else (8, 24)

    return of


def kernel(
    nx, ny, load, modulus, anchor, wall_mask, XC, BK, DG,
    f_load, f_mod, f_anc, mask, INV, XA, SY, RY, SC, RC, SPY, RPY, SPC, RPC,
    ZC, LC, ZR, LH, IDC, PB, PK, Q, CB, CK, CX, CY, RB, RD, PC, RK, R2, RY2, RN, RM2, ZF,
    in_sem, s1, r1, sk, rk, s2, r2, sp, rp, s3, r3,
):
    ix, iy = lax.axis_index("gx"), lax.axis_index("gy")

    def there(d):
        conds = []
        if d[0] < 0:
            conds.append(ix >= -d[0])
        if d[0] > 0:
            conds.append(ix < nx - d[0])
        if d[1] < 0:
            conds.append(iy >= -d[1])
        if d[1] > 0:
            conds.append(iy < ny - d[1])
        return functools.reduce(jnp.logical_and, conds)

    def device(d):
        return (ix + d[0], iy + d[1])

    def opposite(d):
        return (-d[0], -d[1])

    barrier = pltpu.get_barrier_semaphore()
    for d in NEAR:

        @pl.when(there(d))
        def _():
            pl.semaphore_signal(barrier, inc=1, device_id=device(d), device_id_type=MESH)

    fetch = [
        pltpu.make_async_copy(modulus, f_mod, in_sem.at[0]),
        pltpu.make_async_copy(anchor, f_anc, in_sem.at[1]),
        pltpu.make_async_copy(wall_mask, mask, in_sem.at[2]),
        pltpu.make_async_copy(load, f_load, in_sem.at[3]),
    ]
    for copy in fetch:
        copy.start()

    def lo_hi(s):
        return 0 if s < 0 else 1

    def first_from(d):
        if d[1] == 0:
            return BK.at[:, 1:4, 8:24, :] if d[0] < 0 else BK.at[:, 20:23, 8:24, :]
        if d[0] == 0:
            return RY.at[lo_hi(d[1])]
        return RC.at[2 * lo_hi(d[0]) + lo_hi(d[1])]

    def first_to(d):
        if d[1] == 0:
            return BK.at[:, 4:7, 8:24, :] if d[0] < 0 else BK.at[:, 17:20, 8:24, :]
        if d[0] == 0:
            return SY.at[lo_hi(d[1])]
        return SC.at[2 * lo_hi(d[0]) + lo_hi(d[1])]

    def pre_from(d):
        if d[1] == 0:
            return XC.at[:, 0:3, 8:24, :] if d[0] < 0 else XC.at[:, 21:24, 8:24, :]
        if d[0] == 0:
            return RPY.at[lo_hi(d[1])]
        return RPC.at[2 * lo_hi(d[0]) + lo_hi(d[1])]

    def pre_to(d):
        if d[1] == 0:
            return XC.at[:, 5:8, 8:24, :] if d[0] < 0 else XC.at[:, 16:19, 8:24, :]
        if d[0] == 0:
            return SPY.at[lo_hi(d[1])]
        return SPC.at[2 * lo_hi(d[0]) + lo_hi(d[1])]

    def stiff_from(d):
        if d[0] == 0:
            return CK.at[10:14, 8:16, :] if d[1] < 0 else CK.at[10:14, 24:32, :]
        return RK.at[lo_hi(d[0]), d[1] + 1]

    def stiff_to(d):
        return PK

    def coarse_from(d):
        if abs(d[0]) < 2 and abs(d[1]) < 2:
            if d[0] == 0:
                return CB.at[:, 10:14, 8:16, :] if d[1] < 0 else CB.at[:, 10:14, 24:32, :]
            return RB.at[lo_hi(d[0])] if d[1] == 0 else RD.at[lo_hi(d[0]), lo_hi(d[1]), 0:2]
        if d[1] == 0:
            return R2.at[lo_hi(d[0])]
        if d[0] == 0:
            return RY2.at[lo_hi(d[1])]
        if abs(d[0]) == 2:
            return RN.at[lo_hi(d[0]), lo_hi(d[1])]
        return RM2.at[lo_hi(d[0]), lo_hi(d[1])]

    def coarse_to(d):
        if abs(d[0]) < 2 and abs(d[1]) < 2:
            return PB if d[0] == 0 or d[1] == 0 else PC.at[lo_hi(d[0]), lo_hi(d[1]), 0:2]
        if d[1] == 0:
            return PB.at[:, 0]
        if d[0] == 0:
            return Q.at[lo_hi(d[1])]
        return Q.at[lo_hi(d[1]), 0]

    def early_from(d):
        return RD.at[lo_hi(d[0]), lo_hi(d[1]), 2]

    def early_to(d):
        return PC.at[lo_hi(d[0]), lo_hi(d[1]), 2]

    def exchange(partners, to, came, send, recv):
        def copy(k, d):
            return pltpu.make_async_remote_copy(
                src_ref=to(d), dst_ref=came(opposite(d)), send_sem=send.at[k], recv_sem=recv.at[k],
                device_id=device(d), device_id_type=MESH,
            )

        def start():
            for k, d in enumerate(partners):

                @pl.when(there(d))
                def _():
                    copy(k, d).start()

        def wait(chosen=lambda d: True):
            for k, d in enumerate(partners):
                if not chosen(d):
                    continue

                @pl.when(there(opposite(d)))
                def _():
                    copy(k, d).wait_recv()

        def drain():
            for k, d in enumerate(partners):

                @pl.when(there(d))
                def _():
                    copy(k, d).wait_send()

        return start, wait, drain

    one = exchange(NEAR, first_to, first_from, s1, r1)
    pre = exchange(NEAR, pre_to, pre_from, sp, rp)
    kay = exchange(NEAR, stiff_to, stiff_from, sk, rk)
    two = exchange(ALL, coarse_to, coarse_from, s2, r2)
    early = exchange(NEAR[:4], early_to, early_from, s3, r3)

    for partners, came in ((NEAR, first_from), (NEAR, pre_from), (NEAR, stiff_from), (ALL, coarse_from), (NEAR[:4], early_from)):
        for d in partners:

            @pl.when(jnp.logical_not(there(d)))
            def _():
                place = came(d)
                place[...] = jnp.zeros(place.shape, jnp.float32)

    spread = (
        lax.broadcasted_iota(jnp.int32, (16, 128), 1) // 8 == lax.broadcasted_iota(jnp.int32, (16, 128), 0)
    ).astype(jnp.float32)
    rows4 = (
        lax.broadcasted_iota(jnp.int32, (16, 4), 0) // 4 == lax.broadcasted_iota(jnp.int32, (16, 4), 1)
    ).astype(jnp.float32)
    fetch[0].wait()
    fetch[1].wait()
    fetch[2].wait()
    for b in range(4):
        wall = jnp.dot(mask[b].astype(jnp.float32), spread, preferred_element_type=jnp.float32)
        wall = jnp.dot(rows4, wall, preferred_element_type=jnp.float32)
        for x in range(4 * b, 4 * b + 4):
            stiff = f_mod[x] * (0.2 + wall)
            diag = f_anc[x] + 6.0 * stiff
            inv = 1.0 / diag
            DG[x] = diag
            INV[x] = inv
            BK[3, 4 + x, 8:24, :] = stiff * inv
            f_mod[x] = stiff
    fetch[3].wait()
    for x in range(16):
        BK[0:3, 4 + x, 8:24, :] = f_load[:, x] * INV[x][None]
    for x in range(16):
        SY[0, :, x] = BK[:, 4 + x, 8:12, :]
        SY[1, :, x] = BK[:, 4 + x, 20:24, :]
    for cx, x0 in ((0, 4), (1, 18)):
        SC[2 * cx] = BK[:, x0 : x0 + 2, 8:12, :]
        SC[2 * cx + 1] = BK[:, x0 : x0 + 2, 20:24, :]

    pl.semaphore_wait(barrier, sum(there(d).astype(jnp.int32) for d in NEAR))
    one[0]()

    pair_sum = 0.125 * (
        lax.broadcasted_iota(jnp.int32, (256, 128), 0) // 2 == lax.broadcasted_iota(jnp.int32, (256, 128), 1)
    ).astype(jnp.float32)

    def gather_pairs(place, lhs, f, cells=range(8)):
        for c in cells:
            v = place[f, c, pl.ds(0, 8, 2), :] + place[f, c, pl.ds(1, 8, 2), :]
            if c < 4:
                lhs[f, c, :, 0:128] = v
            else:
                lhs[f, 7 - c, :, 128:256] = v

    def boxes(lhs):
        flat = lhs.reshape(-1, 256)
        return jnp.dot(flat, pair_sum, precision=lax.Precision.HIGHEST, preferred_element_type=jnp.float32)

    for c in range(8):
        ZC[0, c] = f_mod[2 * c] + f_mod[2 * c + 1]
        ZC[1, c] = f_anc[2 * c] + f_anc[2 * c + 1]
    gather_pairs(ZC, LC, 0)
    gather_pairs(ZC, LC, 1)
    means = boxes(LC[...])
    coarse_stiff = 0.25 * means[0:32]
    inv = 1.0 / (means[32:64] + 6.0 * coarse_stiff)
    IDC[...] = inv.reshape(4, 8, 128)
    coarse_k = (coarse_stiff * inv).reshape(4, 8, 128)
    PK[...] = coarse_k
    CK[10:14, 16:24, :] = coarse_k
    kay[0]()

    ends = lane_ends(128)
    theta, ((a1, b1), (a2, b2)) = rates(0.5, 2.0, SMOOTH)

    def fine_k(x, r0, n):
        return BK[3, x, r0 : r0 + n, :]

    def smooth(second, third, pairs):
        coefs = ((1.0 + a1 - b1) / theta + b1, b1 / theta, 0.0, 0.0)
        for planes in second:
            sweep(XA, BK, None, BK, fine_k, coefs, planes, fine_rows(2), ends)
        coefs = (1.0 + a2 - b2, b2, b2 - a2 / theta, 0.0)
        for planes in third:
            sweep(XC, XA, None, BK, fine_k, coefs, planes, fine_rows(1), ends)
        held = {}
        for c in pairs:
            total = 0.0
            for x in (4 + 2 * c, 5 + 2 * c):
                v, nb = around(XC, x, (8, 16), ends, held)
                total = total + DG[x - 4][None] * (BK[0:3, x, 8:24, :] - v + fine_k(x, 8, 16)[None] * nb)
            ZR[:, c] = total

    one[1](lambda d: d[0] == 0)
    for x in range(16):
        BK[:, 4 + x, 4:8, :] = RY[0, :, x]
        BK[:, 4 + x, 24:28, :] = RY[1, :, x]
    smooth([range(5, 19)], [range(6, 18)], range(2, 6))
    left = lax.broadcasted_iota(jnp.int32, (8, 128), 1) < 64
    row = lax.broadcasted_iota(jnp.int32, (8, 128), 0)
    for f in range(3):
        gather_pairs(ZR, LH, f, range(2, 6))
    inner = boxes(LH[:, 2:4]).reshape(3, 2, 8, 128) * IDC[2:4][None]
    PB[:, 2:4] = inner
    for dx in (0, 1):
        far_half = left if dx else jnp.logical_not(left)
        for dy in (0, 1):
            PC[dx, dy, 2] = jnp.where(far_half, pltpu.roll(inner[:, 1], 64, 2), inner[:, 0])
    early[0]()
    one[1](lambda d: d[0] != 0)
    for cx, x0 in ((0, 2), (1, 20)):
        BK[:, x0 : x0 + 2, 4:8, :] = RC[2 * cx]
        BK[:, x0 : x0 + 2, 24:28, :] = RC[2 * cx + 1]
    smooth([range(2, 5), range(19, 22)], [range(3, 6), range(18, 21)], (0, 1, 6, 7))

    for f in range(3):
        gather_pairs(ZR, LH, f, (0, 1, 6, 7))
    outer = boxes(LH[:, 0:2]).reshape(3, 2, 8, 128) * IDC[0:2][None]
    PB[:, 0:2] = outer
    rest = [outer[:, 0], outer[:, 1], inner[:, 0], inner[:, 1]]
    for dx in (0, 1):
        far_half = left if dx else jnp.logical_not(left)
        first_two = jnp.where(far_half, pltpu.roll(rest[1], 64, 2), rest[0])
        for dy, shift1, shift0, has1, has0 in ((0, 5, 6, row >= 5, row >= 6), (1, 3, 2, row < 3, row < 2)):
            odd = jnp.where(has1, pltpu.roll(rest[1], shift1, 1), rest[3])
            even = jnp.where(has0, pltpu.roll(rest[0], shift0, 1), rest[2])
            PC[dx, dy, 0] = first_two
            PC[dx, dy, 1] = jnp.where(far_half, odd, pltpu.roll(even, 64, 2))
    for j in range(4):
        Q[0, j, 0:3] = rest[j][:, 0, :]
        Q[1, j, 0:3] = rest[j][:, 7, :]
    two[0]()
    CB[:, 10:14, 16:24, :] = PB[...]

    for x in range(16):
        SPY[0, :, x] = XC[:, 4 + x, 8:12, :]
        SPY[1, :, x] = XC[:, 4 + x, 20:24, :]
    for cx, x0 in ((0, 4), (1, 17)):
        SPC[2 * cx] = XC[:, x0 : x0 + 3, 8:12, :]
        SPC[2 * cx + 1] = XC[:, x0 : x0 + 3, 20:24, :]
    pre[0]()

    def meet(lo, hi):
        return pltpu.roll(jnp.where(left[: lo.shape[-2]], hi, lo), 64, lo.ndim - 1)

    kay[1]()
    for y in range(3):
        rows = slice(8 + 8 * y, 16 + 8 * y)
        for j in range(4):
            lo, hi = RK[0, y, j], RK[1, y, j]
            CK[2 + j, rows, :] = jnp.where(left, lo, hi)
            CK[9 - j, rows, :] = meet(lo, hi)
    early[1]()
    two[1]()
    for j in range(4):
        lo, hi = RB[0, :, j], RB[1, :, j]
        CB[:, 2 + j, 16:24, :] = jnp.where(left, lo, hi)
        CB[:, 9 - j, 16:24, :] = meet(lo, hi)
    for y, rows, back1, back0 in ((0, slice(8, 16), 5, 6), (1, slice(24, 32), 3, 2)):
        for part in (0, 1):
            lo, hi = RD[0, y, 2 * part], RD[1, y, 2 * part]
            CB[:, 9 - 2 * part, rows, :] = meet(lo, hi)
            CB[:, 8 - 2 * part, rows, :] = jnp.where(left, lo, hi)
        odd, even = jnp.where(left, RD[0, y, 1], RD[1, y, 1]), meet(RD[0, y, 1], RD[1, y, 1])
        CB[:, 5, rows, :] = odd
        CB[:, 3, rows, :] = pltpu.roll(odd, back1, 1)
        CB[:, 4, rows, :] = even
        CB[:, 2, rows, :] = pltpu.roll(even, back0, 1)
    for f in range(3):
        CB[f, 1, 16:24, :] = meet(R2[0, f], R2[1, f])
    for y, near, far in ((0, 15, 7), (1, 24, 32)):
        near_row = meet(RN[0, y, 0:3], RN[1, y, 0:3])
        far_row = meet(RM2[0, y, 0:3], RM2[1, y, 0:3])
        for f in range(3):
            CB[f, 1, near : near + 1, :] = near_row[f : f + 1]
            CB[f, 9, far : far + 1, :] = far_row[f : f + 1]
            for j in range(4):
                CB[f, 10 + j, far : far + 1, :] = RY2[y, j, f : f + 1]

    ends_c = lane_ends(64)
    theta_c, steps = rates(0.05, 2.0, COARSE_STEPS)

    def coarse_k_at(x, r0, n):
        return CK[x, r0 : r0 + n, :]

    at = CB
    for t in range(2, COARSE_STEPS + 1):
        a, b = steps[t - 2]
        to = CY if t % 2 == 0 else CX
        if t == 2:
            coefs, prev = ((1.0 + a - b) / theta_c + b, b / theta_c, 0.0, 0.0), None
        elif t == 3:
            coefs, prev = (1.0 + a - b, b, b - a / theta_c, 0.0), None
        else:
            coefs, prev = (1.0 + a - b, b, b, -a), to
        sweep(to, at, prev, CB, coarse_k_at, coefs, range(t, 14), coarse_rows(t), ends_c, 13)
        at = to

    repeat = (
        lax.broadcasted_iota(jnp.int32, (128, 256), 1) // 2 == lax.broadcasted_iota(jnp.int32, (128, 256), 0)
    ).astype(jnp.bfloat16)
    pre[1]()
    pre[2]()
    for x in range(16):
        XC[:, 4 + x, 4:8, :] = RPY[0, :, x]
        XC[:, 4 + x, 24:28, :] = RPY[1, :, x]
    for cx, x0 in ((0, 1), (1, 20)):
        XC[:, x0 : x0 + 3, 4:8, :] = RPC[2 * cx]
        XC[:, x0 : x0 + 3, 24:28, :] = RPC[2 * cx + 1]
    for f in range(3):
        for i in range(6):
            v = at[f, 8 + i, 14:26, :]
            ZF[f, i, pl.ds(0, 12, 2), :] = v
            ZF[f, i, pl.ds(1, 12, 2), :] = v
        whole = ZF[f].reshape(144, 128)
        up = 0.0
        for _ in range(3):
            piece = whole.astype(jnp.bfloat16)
            up = up + jnp.dot(piece, repeat, preferred_element_type=jnp.float32)
            whole = whole - piece.astype(jnp.float32)
        up = up.reshape(6, 24, 256)
        for i in range(6):
            for x, v in ((2 * i, up[i, :, 0:128]), (22 - 2 * i, up[i, :, 128:256])):
                XC[f, x, 4:28, :] = XC[f, x, 4:28, :] + v
                XC[f, x + 1, 4:28, :] = XC[f, x + 1, 4:28, :] + v
    for _, _, drain in (one, kay, early, two):
        drain()


def after(XC, BK, DG, out_sol, out_rem, XA, XB, RM, out_sem):
    ends = lane_ends(128)
    theta, ((a1, b1), (a2, b2)) = rates(0.5, 2.0, SMOOTH)

    def fine_k(x, r0, n):
        return BK[3, x, r0 : r0 + n, :]

    sweep(XA, XC, None, BK, fine_k, (1.0 - 1.0 / theta, 1.0 / theta, 1.0 / theta, 0.0), range(1, 23), fine_rows(3), ends)
    sweep(XB, XA, XC, BK, fine_k, (1.0 + a1 - b1, b1, b1, -a1), range(2, 22), fine_rows(2), ends)
    sweep(XA, XB, XA, BK, fine_k, (1.0 + a2 - b2, b2, b2, -a2), range(3, 21), fine_rows(1), ends)
    put = [
        pltpu.make_async_copy(XA.at[:, 4:20, 8:24, :], out_sol, out_sem.at[0]),
        *(
            pltpu.make_async_copy(RM.at[:, a : a + 4], out_rem.at[:, a : a + 4], out_sem.at[1 + a // 4])
            for a in range(0, 16, 4)
        ),
    ]
    put[0].start()
    held = {}
    for x in range(4, 20):
        v, nb = around(XA, x, (8, 16), ends, held)
        RM[:, x - 4] = DG[x - 4][None] * (BK[0:3, x, 8:24, :] - v + fine_k(x, 8, 16)[None] * nb)
        if x % 4 == 3:
            put[x // 4].start()
    for copy in put:
        copy.wait()


def local(nx, ny, load, modulus, anchor, wall_mask):
    f32 = jnp.float32

    def vmem(*shape):
        return pltpu.VMEM(shape, f32)

    dma = pltpu.SemaphoreType.DMA
    far = pl.BlockSpec(memory_space=pltpu.HBM)
    near = pl.BlockSpec(memory_space=pltpu.VMEM)
    inner = pl.pallas_call(
        functools.partial(kernel, nx, ny),
        out_shape=(
            jax.ShapeDtypeStruct((3, 24, 32, 128), f32),
            jax.ShapeDtypeStruct((4, 24, 32, 128), f32),
            jax.ShapeDtypeStruct((16, 16, 128), f32),
        ),
        in_specs=[far] * 4,
        out_specs=(near, near, near),
        scratch_shapes=[
            vmem(3, 16, 16, 128), vmem(16, 16, 128), vmem(16, 16, 128),
            pltpu.VMEM((4, 4, 16), jnp.int32), vmem(16, 16, 128), vmem(3, 24, 32, 128),
            vmem(2, 4, 16, 4, 128), vmem(2, 4, 16, 4, 128), vmem(4, 4, 2, 4, 128), vmem(4, 4, 2, 4, 128),
            vmem(2, 3, 16, 4, 128), vmem(2, 3, 16, 4, 128), vmem(4, 3, 3, 4, 128), vmem(4, 3, 3, 4, 128),
            vmem(2, 8, 16, 128), vmem(2, 4, 8, 256), vmem(3, 8, 16, 128), vmem(3, 4, 8, 256),
            vmem(4, 8, 128), vmem(3, 4, 8, 128), vmem(4, 8, 128), vmem(2, 4, 4, 128),
            vmem(3, 14, 40, 128), vmem(14, 40, 128), vmem(3, 14, 40, 128), vmem(3, 14, 40, 128),
            vmem(2, 3, 4, 8, 128), vmem(2, 2, 3, 3, 8, 128), vmem(2, 2, 3, 3, 8, 128),
            vmem(2, 3, 4, 8, 128), vmem(2, 3, 8, 128),
            vmem(2, 4, 4, 128), vmem(2, 2, 4, 128), vmem(2, 2, 4, 128),
            vmem(3, 6, 24, 128),
            dma((4,)), dma((8,)), dma((8,)), dma((8,)), dma((8,)), dma((20,)), dma((20,)), dma((8,)), dma((8,)), dma((4,)), dma((4,)),
        ],
        compiler_params=pltpu.CompilerParams(collective_id=0, has_side_effects=True, vmem_limit_bytes=24 << 20),
    )(*(pltpu.with_memory_space_constraint(a, pltpu.HBM) for a in (load, modulus, anchor, wall_mask)))
    shape = jax.ShapeDtypeStruct((3, 16, 16, 128), f32)
    return pl.pallas_call(
        after,
        out_shape=(shape, shape),
        in_specs=[near] * 3,
        out_specs=(far, far),
        scratch_shapes=[vmem(3, 24, 32, 128), vmem(3, 24, 32, 128), vmem(3, 16, 16, 128), dma((5,))],
        compiler_params=pltpu.CompilerParams(vmem_limit_bytes=16 << 20),
    )(*inner)


def solution(mesh):
    return jax.shard_map(
        functools.partial(local, mesh.shape["gx"], mesh.shape["gy"]),
        mesh=mesh,
        in_specs=(
            P(None, "gx", "gy", None),
            P("gx", "gy", None),
            P("gx", "gy", None),
            P("gx", "gy", None),
        ),
        out_specs=(P(None, "gx", "gy", None), P(None, "gx", "gy", None)),
        check_vma=False,
    )
```
